512 devices in a mesh: dp: 256 (over z_hi, y, x, core), mp: 2 (over z_lo).
Axes of the slice: x: 4, y: 8, z: 8 (z_hi: 4, z_lo: 2; z = z_hi * 2 + z_lo), core: 2. Of those that a mesh axis runs over, the one named last changes fastest.
Arguments:
- visual_encoder_outputs: bfloat16 [65536, 1152], P('dp'), may hold values from -6 to 6
- visual_mapping_matrix: bfloat16 [1152, 1152], P(None, 'mp'), may hold values from -0.1875 to 0.1875
- sentence_vectors_raw: bfloat16 [65536, 1152], P('dp', 'mp'), may hold values from -0.1796875 to 0.1796875
- matched_sentence_rows: int32 [65536], P('dp'), may hold values from 0 to 65535, as said below
- sharpness_coefficient: float32 [1], replicated, may hold values from 5 to 15
- pairwise_offset: float32 [1], replicated, may hold values from -4 to -1
Outputs:
- loss: float32 [1], replicated
- proj_grad: bfloat16 [1152, 1152], P(None, 'mp')
- caption_gradient: bfloat16 [65536, 1152], P('dp', 'mp')
The draws below stay inside these ranges and needn't reach their ends.
Inputs may be any that keep to these rules, and one draw needn't show every extreme that they name: `matched_sentence_rows`: the matching text row of an image row in block b lies in block (b - s) mod 256 for some s of 0 .. 2, blocks of 256 rows.
All inputs are finite; a program needn't handle non-finite values.
Results may differ from the reference program's by a relative error of at most 0.014.
Values may be sent and summed in bfloat16 or wider, within the bound.
A program may use at most 64 MiB of HBM per device.

```python
import jax
import jax.numpy as jnp
from jax import lax

D = 1152
E = 1152
TOK_DEV = 256
STEPS = 2
TOKENS = 65536
N_DP = 256


def draw_matched_sentence_rows(key, part):
    key = jax.random.fold_in(key, 7)
    first, second = jax.random.split(key)
    rows = jnp.arange(TOKENS, dtype=jnp.int32)
    blocks = TOKENS // TOK_DEV
    back = jax.random.randint(first, (TOKENS,), 0, STEPS + 1, dtype=jnp.int32)
    within = jax.random.randint(second, (TOKENS,), 0, TOK_DEV, dtype=jnp.int32)
    back = jnp.where(rows == 0, 1, jnp.where(rows == 1, 0, back))
    within = jnp.where(rows == 0, TOK_DEV - 1, jnp.where(rows == 1, 0, within))
    owner = (rows // TOK_DEV - back) % blocks
    return (owner * TOK_DEV + within).astype(jnp.int32)


def steps_of(rng, extent, cuts, smallest, high):
    gain, own = 1.0, jax.random.fold_in(rng, 6)
    for dim, blocks in cuts:
        heights = jnp.exp(jax.random.uniform(jax.random.fold_in(own, dim), (blocks,), jnp.float32, smallest / len(cuts), high / len(cuts)))
        gain = gain * jnp.repeat(heights, extent[dim] // blocks).reshape([-1 if axis == dim else 1 for axis in range(len(extent))])
    return gain


def centred(own_key, extent, scale, bound, pieces=(), kind=jnp.bfloat16):
    values = jax.random.normal(own_key, extent, jnp.float32) * scale
    if len(pieces) > 0:
        values = steps_of(own_key, extent, pieces, -0.22, 0.18) * values
    return jnp.clip(values, min=-bound, max=bound).astype(kind)


def setup_inputs(seed: int = 0) -> dict:
    key_list = jax.random.split(jax.random.key(seed), 7)
    return {
        "visual_encoder_outputs": centred(key_list[0], (TOKENS, D), 1.0, 6.0, ((0, 256),)),
        "visual_mapping_matrix": centred(key_list[1], (D, E), D ** -0.5, 0.1875, ((1, 2),)),
        "sentence_vectors_raw": centred(key_list[2], (TOKENS, E), 0.03, 0.1796875, ((0, 256), (1, 2))),
        "matched_sentence_rows": draw_matched_sentence_rows(jax.random.fold_in(key_list[6], 71), 0),
        "sharpness_coefficient": jnp.clip(jax.random.uniform(key_list[4], (1,), jnp.float32, 5.0, 15.0), 5.0, 15.0),
        "pairwise_offset": jnp.clip(jax.random.uniform(key_list[5], (1,), jnp.float32, -4.0, -1.0), -4.0, -1.0),
    }


epsilon = 1e-06

def unit_rows(values):
    norms = jnp.sqrt(lax.optimization_barrier(jnp.sum(values * values, axis=1, keepdims=True)) + epsilon)
    return (values / norms, norms)

def reference(visual_encoder_outputs, visual_mapping_matrix, sentence_vectors_raw, matched_sentence_rows, sharpness_coefficient, pairwise_offset):
    image_raw = jnp.dot(visual_encoder_outputs, visual_mapping_matrix, preferred_element_type=jnp.float32)
    image_unit, image_norm = unit_rows(image_raw)
    image_low = image_unit.astype(jnp.bfloat16)
    text_unit, text_norm = unit_rows(sentence_vectors_raw.astype(jnp.float32))
    text_low = text_unit.astype(jnp.bfloat16)
    similarity_multiplier = sharpness_coefficient[0]
    offset_b = pairwise_offset[0]
    columns = jnp.arange(TOK_DEV, dtype=jnp.int32)

    def per_block(text_direction, source):
        start = (source * TOK_DEV).astype(jnp.int32)
        image_block = lax.dynamic_slice_in_dim(image_low, start, TOK_DEV, 0)
        pos_block = lax.dynamic_slice_in_dim(matched_sentence_rows, start, TOK_DEV, 0)
        image_direction = jnp.zeros((TOK_DEV, E), jnp.float32)
        loss_part = jnp.zeros((), jnp.float32)
        for stride in range(STEPS + 1):
            owner = ((source - stride) % N_DP).astype(jnp.int32)
            text_start = (owner * TOK_DEV).astype(jnp.int32)
            text_block = lax.dynamic_slice_in_dim(text_low, text_start, TOK_DEV, 0)
            ids = text_start + columns
            logits = similarity_multiplier * lax.dot_general(image_block, text_block, (((1,), (1,)), ((), ())), preferred_element_type=jnp.float32) + offset_b
            signs = jnp.where(pos_block[:, None] == ids[None, :], 1.0, -1.0).astype(jnp.float32)
            loss_part = loss_part + jnp.sum(jax.nn.softplus(-signs * logits))
            weight = (-signs * jax.nn.sigmoid(-signs * logits) * similarity_multiplier).astype(jnp.bfloat16)
            image_direction = image_direction + jnp.dot(weight, text_block, preferred_element_type=jnp.float32)
            text_part = lax.dot_general(weight, image_block, (((0,), (0,)), ((), ())), preferred_element_type=jnp.float32)
            old = lax.dynamic_slice_in_dim(text_direction, text_start, TOK_DEV, 0)
            text_direction = lax.dynamic_update_slice_in_dim(text_direction, old + text_part, text_start, 0)
        return (text_direction, (image_direction, loss_part))
    text_direction, (image_dirs, loss_parts) = lax.scan(per_block, jnp.zeros((TOKENS, E), jnp.float32), jnp.arange(N_DP, dtype=jnp.int32))
    image_direction = image_dirs.reshape(TOKENS, E)
    loss = (jnp.sum(loss_parts) / TOKENS).reshape(1)
    image_back = ((image_direction - image_unit * lax.optimization_barrier(jnp.sum(image_unit * image_direction, axis=1, keepdims=True))) / image_norm).astype(jnp.bfloat16)
    proj_grad = lax.dot_general(visual_encoder_outputs, image_back, (((0,), (0,)), ((), ())), preferred_element_type=jnp.float32).astype(jnp.bfloat16)
    caption_gradient = ((text_direction - text_unit * lax.optimization_barrier(jnp.sum(text_unit * text_direction, axis=1, keepdims=True))) / text_norm).astype(jnp.bfloat16)
    return (loss, proj_grad, caption_gradient)
```

```python
import functools

import jax
import jax.numpy as jnp
from jax import lax
from jax.experimental import pallas as pl
from jax.experimental.pallas import tpu as pltpu
from jax.sharding import PartitionSpec as P

STEPS = 2
NX, NY, NZ = 4, 8, 4
BLOCKS = NX * NY * NZ * 2
EPSILON = 1e-06
ROW_TILE = 16
LANES = 128
MESH = pl.DeviceIdType.MESH
F32, BF16 = jnp.float32, jnp.bfloat16


def dot(a, b, over_a, over_b):
    return lax.dot_general(a, b, (((over_a,), (over_b,)), ((), ())), preferred_element_type=F32)


def up(value, step):
    return -(-value // step)


def sizes(width, depth):
    full = (width // 2) * (depth // LANES)
    of_x = up(full // ROW_TILE, NX) * ROW_TILE
    of_y = up(of_x // ROW_TILE, NY) * ROW_TILE
    of_z = up(of_y // ROW_TILE, NZ) * ROW_TILE
    return full, of_x, of_y, of_z


class Copies:
    def __init__(self, send_sem, recv_sem):
        self.send_sem, self.recv_sem, self.made = send_sem, recv_sem, []

    def start(self, source, target, device):
        i = len(self.made)
        copy = pltpu.make_async_remote_copy(
            src_ref=source,
            dst_ref=target,
            send_sem=self.send_sem.at[i],
            recv_sem=self.recv_sem.at[i],
            device_id=device,
            device_id_type=MESH,
        )
        copy.start()
        self.made.append(copy)
        return copy


def kernel(
    x_hbm,
    w_hbm,
    t_hbm,
    matched_ref,
    scale_ref,
    offset_ref,
    loss_ref,
    flat_ref,
    cap_ref,
    x_all,
    w_ref,
    text_raw,
    text_low,
    image_unit,
    image_low,
    sums_out,
    sums_in,
    text_sums,
    cos_out,
    cos_in,
    weight,
    back,
    back_all,
    g_x,
    g_y,
    g_z,
    h_z,
    h_y,
    r_x,
    r_y,
    r_z,
    loss_core,
    loss_x,
    loss_y,
    loss_z,
    text_part,
    text_in,
    tdot_out,
    tdot_in,
    load_sem,
    send_sem,
    recv_sem,
):
    width, rows = t_hbm.shape
    depth = x_hbm.shape[1]
    half = width // 2
    full, of_x, of_y, of_z = sizes(width, depth)
    dp, mp = lax.axis_index("dp"), lax.axis_index("mp")
    core = lax.rem(dp, 2)
    x = lax.rem(dp // 2, NX)
    y = lax.rem(dp // (2 * NX), NY)
    z = dp // (2 * NX * NY)
    other_mp = (dp, 1 - mp)
    other_core = (dp + 1 - 2 * core, mp)

    def along_dp(step):
        return (lax.rem(dp + step + BLOCKS, BLOCKS), mp)

    def along(count, at, stride):
        places = [lax.rem(at + k, count) for k in range(1, count)]
        return [(place, (dp + (place - at) * stride, mp)) for place in places]

    def source_of(count, at, k):
        return lax.rem(at - k + count, count)

    on_x, on_y, on_z = along(NX, x, 2), along(NY, y, 2 * NX), along(NZ, z, 2 * NX * NY)

    loads = [
        pltpu.make_async_copy(t_hbm, text_raw.at[0], load_sem.at[0]),
        pltpu.make_async_copy(w_hbm, w_ref, load_sem.at[1]),
        pltpu.make_async_copy(x_hbm, x_all.at[core], load_sem.at[2]),
    ]
    for load in loads:
        load.start()

    barrier = pltpu.get_barrier_semaphore()
    greeted = [other_mp, other_core] + [along_dp(s) for s in (-2, -1, 1, 2)]
    greeted += [device for _, device in on_x + on_y + on_z]
    for device in greeted:
        pl.semaphore_signal(barrier, inc=1, device_id=device, device_id_type=MESH)
    pl.semaphore_wait(barrier, len(greeted))

    copies = Copies(send_sem, recv_sem)
    send = copies.start
    text_there = [send(t_hbm, text_raw.at[s], along_dp(s)) for s in (1, 2)]

    for load in loads:
        load.wait()
    x_there = send(x_all.at[core], x_all.at[core], other_core)
    image_raw = dot(w_ref[...], x_all[core], 1, 1)
    own_text = text_raw[0].astype(F32)
    sums_out[0:1, :] = jnp.sum(image_raw * image_raw, axis=0, keepdims=True)
    sums_out[1:2, :] = jnp.sum(own_text * own_text, axis=0, keepdims=True)
    sums_there = send(sums_out, sums_in, other_mp)
    sums_there.wait_recv()
    sums = sums_out[...] + sums_in[...]
    image_scale = lax.rsqrt(sums[0:1, :] + EPSILON)
    text_scale = lax.rsqrt(sums[1:2, :] + EPSILON)
    text_sums[0] = sums
    text_sums_there = [send(text_sums.at[0], text_sums.at[s], along_dp(s)) for s in (1, 2)]
    unit = image_raw * image_scale
    image_unit[...] = unit
    image_low[...] = unit.astype(BF16)

    cos_there = []
    for s in range(STEPS + 1):
        if s > 0:
            text_there[s - 1].wait_recv()
            text_sums_there[s - 1].wait_recv()
            text_low[s] = (
                text_raw[s].astype(F32) * lax.rsqrt(text_sums[s, 1:2, :] + EPSILON)
            ).astype(BF16)
        else:
            text_low[0] = (own_text * text_scale).astype(BF16)
        cos_out[s] = dot(text_low[s], image_low[...], 0, 0).astype(BF16)
        cos_there.append(send(cos_out.at[s], cos_in.at[s], other_mp))

    sharpness, offset = scale_ref[0], offset_ref[0]
    loss_rows = jnp.zeros((1, rows), F32)
    along_unit = jnp.zeros((1, rows), F32)
    direction = jnp.zeros((width, rows), F32)
    for s in range(STEPS + 1):
        cos_there[s].wait_recv()
        cos = cos_out[s].astype(F32) + cos_in[s].astype(F32)
        ids = lax.rem(dp - s + BLOCKS, BLOCKS) * rows + lax.broadcasted_iota(jnp.int32, (rows, rows), 0)
        matched = ids == matched_ref[...]
        logit = sharpness * cos + offset
        against = jnp.where(matched, -logit, logit)
        small = jnp.exp(-jnp.abs(against))
        loss_rows += jnp.sum(jnp.maximum(against, 0.0) + jnp.log1p(small), axis=0, keepdims=True)
        sigmoid = jnp.where(against >= 0.0, 1.0, small) / (1.0 + small)
        low = (jnp.where(matched, -sigmoid, sigmoid) * sharpness).astype(BF16)
        weight[s] = low
        along_unit += jnp.sum(low.astype(F32) * cos, axis=0, keepdims=True)
        direction += dot(text_low[s], low, 1, 0)

    image_back = ((direction - image_unit[...] * along_unit) * image_scale).astype(BF16)
    back[0] = image_back[:half]
    back[1] = image_back[half:]
    back_there = send(back.at[1 - core], back_all.at[core], other_core)
    back_all[core] = back[core]
    lanes = loss_rows[:, : rows // 2] + loss_rows[:, rows // 2 :]
    if rows // 2 < LANES:
        lanes = jnp.concatenate([lanes, jnp.zeros((1, LANES - rows // 2), F32)], axis=1)
    loss_core[core] = jnp.broadcast_to(lanes, (8, LANES))
    loss_core_there = send(loss_core.at[core], loss_core.at[core], other_core)

    x_there.wait_recv()
    back_there.wait_recv()
    mine, others = back_all[core], back_all[1 - core]
    x_mine, x_others = x_all[core], x_all[1 - core]
    for k in range(depth // LANES):
        cols = slice(k * LANES, (k + 1) * LANES)
        part = dot(mine, x_mine[:, cols], 1, 0) + dot(others, x_others[:, cols], 1, 0)
        g_x[k * half : (k + 1) * half, :] = part.astype(BF16)
    if NX * of_x > full:
        g_x[full:, :] = jnp.zeros((NX * of_x - full, LANES), BF16)

    def rows_of(ref, place, count):
        return ref.at[pl.ds(pl.multiple_of(place * count, ROW_TILE), count)]

    def scatter(places, full_ref, count, landing, own_place, loss_landing, loss_now):
        there = [
            send(rows_of(full_ref, place, count), landing.at[k], device)
            for k, (place, device) in enumerate(places)
        ]
        loss_landing[own_place] = loss_now
        loss_sent = [
            send(loss_landing.at[own_place], loss_landing.at[own_place], device)
            for _, device in places
        ]
        return there, loss_sent

    def gather_sum(there, full_ref, count, landing, own_place):
        total = rows_of(full_ref, own_place, count)[...].astype(F32)
        for k, copy in enumerate(there):
            copy.wait_recv()
            total += landing[k].astype(F32)
        return total

    def loss_sum(loss_sent, loss_landing, count):
        for copy in loss_sent:
            copy.wait_recv()
        total = loss_landing[0]
        for k in range(1, count):
            total += loss_landing[k]
        return total

    loss_core_there.wait_recv()
    there, loss_sent = scatter(on_x, g_x, of_x, r_x, x, loss_x, loss_core[0] + loss_core[1])
    own_part = dot(image_low[...], weight[0], 1, 1)
    for s in (1, 2):
        text_part[s - 1] = dot(image_low[...], weight[s], 1, 1).astype(BF16)
    total = gather_sum(there, g_x, of_x, r_x, x)
    g_y[:of_x, :] = total.astype(BF16)
    if NY * of_y > of_x:
        g_y[of_x:, :] = jnp.zeros((NY * of_y - of_x, LANES), BF16)
    loss_now = loss_sum(loss_sent, loss_x, NX)

    there, loss_sent = scatter(on_y, g_y, of_y, r_y, y, loss_y, loss_now)
    parts_there = [send(text_part.at[s - 1], text_in.at[s - 1], along_dp(-s)) for s in (1, 2)]
    total = gather_sum(there, g_y, of_y, r_y, y)
    g_z[:of_y, :] = total.astype(BF16)
    if NZ * of_z > of_y:
        g_z[of_y:, :] = jnp.zeros((NZ * of_z - of_y, LANES), BF16)
    loss_now = loss_sum(loss_sent, loss_y, NY)

    there, loss_sent = scatter(on_z, g_z, of_z, r_z, z, loss_z, loss_now)
    total = gather_sum(there, g_z, of_z, r_z, z)
    own_z = rows_of(h_z, z, of_z)
    own_z[...] = total.astype(BF16)

    there = [send(own_z, own_z, device) for _, device in on_z]
    loss_now = loss_sum(loss_sent, loss_z, NZ)
    loss_ref[0] = jnp.sum(loss_now[0:1, :]) / (rows * BLOCKS)
    for copy in there:
        copy.wait_recv()
    own_y = rows_of(h_y, y, of_y)
    own_y[...] = h_z[:of_y, :]
    there = [send(own_y, own_y, device) for _, device in on_y]

    for copy in parts_there:
        copy.wait_recv()
    text_dir = own_part + text_in[0].astype(F32) + text_in[1].astype(F32)
    text_unit = text_raw[0].astype(F32) * text_scale
    tdot = jnp.sum(text_unit * text_dir, axis=0, keepdims=True)
    tdot_out[...] = jnp.broadcast_to(tdot, tdot_out.shape)
    tdot_there = send(tdot_out, tdot_in, other_mp)

    for copy in there:
        copy.wait_recv()

    def chunk(place):
        return flat_ref.at[core, pl.ds(pl.multiple_of(place * of_x, ROW_TILE), of_x)]

    chunk(x)[...] = h_y[:of_x, :]
    there = [send(chunk(x), chunk(x), device) for _, device in on_x]
    relayed = [send(chunk(x), chunk(x), other_core)]
    tdot_there.wait_recv()
    tdot = tdot_out[0:1, :] + tdot_in[0:1, :]
    cap_ref[...] = ((text_dir - text_unit * tdot) * text_scale).astype(BF16)
    for k, copy in enumerate(there):
        copy.wait_recv()
        place = source_of(NX, x, k + 1)
        relayed.append(send(chunk(place), chunk(place), other_core))
    for copy in relayed:
        copy.wait_recv()
    for copy in copies.made:
        copy.wait_send()


def local(x_rows, w_half, t_half, matched, sharpness, offset):
    rows, depth = x_rows.shape
    width = w_half.shape[1]
    half = width // 2
    full, of_x, of_y, of_z = sizes(width, depth)
    n_copies = 2 + 1 + 1 + 2 + 3 + 2 + 3 * (NX + NY + NZ - 3) + 2 + 1 + 1 + (NX - 1)
    vmem, whole = pl.BlockSpec(memory_space=pltpu.VMEM), pl.BlockSpec(memory_space=pl.ANY)
    smem = pl.BlockSpec(memory_space=pltpu.SMEM)
    flat_shape = (2, NX * of_x, LANES)
    call = pl.pallas_call(
        kernel,
        out_shape=(
            jax.ShapeDtypeStruct((1,), F32),
            jax.ShapeDtypeStruct(flat_shape, BF16),
            jax.ShapeDtypeStruct((width, rows), BF16),
        ),
        in_specs=[whole, whole, whole, vmem, smem, smem],
        out_specs=(smem, vmem, vmem),
        scratch_shapes=[
            pltpu.VMEM((2, rows, depth), BF16),
            pltpu.VMEM((width, depth), BF16),
            pltpu.VMEM((3, width, rows), BF16),
            pltpu.VMEM((3, width, rows), BF16),
            pltpu.VMEM((width, rows), F32),
            pltpu.VMEM((width, rows), BF16),
            pltpu.VMEM((8, rows), F32),
            pltpu.VMEM((8, rows), F32),
            pltpu.VMEM((3, 8, rows), F32),
            pltpu.VMEM((3, rows, rows), BF16),
            pltpu.VMEM((3, rows, rows), BF16),
            pltpu.VMEM((3, rows, rows), BF16),
            pltpu.VMEM((2, half, rows), BF16),
            pltpu.VMEM((2, half, rows), BF16),
            pltpu.VMEM((NX * of_x, LANES), BF16),
            pltpu.VMEM((NY * of_y, LANES), BF16),
            pltpu.VMEM((NZ * of_z, LANES), BF16),
            pltpu.VMEM((NZ * of_z, LANES), BF16),
            pltpu.VMEM((NY * of_y, LANES), BF16),
            pltpu.VMEM((NX - 1, of_x, LANES), BF16),
            pltpu.VMEM((NY - 1, of_y, LANES), BF16),
            pltpu.VMEM((NZ - 1, of_z, LANES), BF16),
            pltpu.VMEM((2, 8, LANES), F32),
            pltpu.VMEM((NX, 8, LANES), F32),
            pltpu.VMEM((NY, 8, LANES), F32),
            pltpu.VMEM((NZ, 8, LANES), F32),
            pltpu.VMEM((2, width, rows), BF16),
            pltpu.VMEM((2, width, rows), BF16),
            pltpu.VMEM((8, rows), F32),
            pltpu.VMEM((8, rows), F32),
            pltpu.SemaphoreType.DMA((3,)),
            pltpu.SemaphoreType.DMA((n_copies,)),
            pltpu.SemaphoreType.DMA((n_copies,)),
        ],
        compiler_params=pltpu.CompilerParams(
            collective_id=0, has_side_effects=True, vmem_limit_bytes=40 * 1024 * 1024
        ),
    )
    loss, flat, cap = call(
        x_rows, w_half.T, t_half.T, matched.reshape(1, rows), sharpness, offset
    )
    tiles = flat[:, :full].reshape(2, depth // LANES, half, LANES)
    grad = tiles.transpose(0, 2, 1, 3).reshape(width, depth)
    return (loss, grad.T, cap.T)


def solution(mesh):
    placed = (P("dp", None), P(None, "mp"), P("dp", "mp"), P("dp"), P(), P())
    return jax.shard_map(
        local,
        mesh=mesh,
        in_specs=placed,
        out_specs=(P(), P(None, "mp"), P("dp", "mp")),
        check_vma=False,
    )
```

```python
import jax
import jax.numpy as jnp
from jax import lax
from jax.experimental import pallas as pl
from jax.experimental.pallas import tpu as pltpu
from jax.sharding import PartitionSpec as P

STEPS = 2
NX, NY, NZ = 4, 8, 4
BLOCKS = NX * NY * NZ * 2
EPSILON = 1e-06
ROW_TILE = 16
LANES = 128
N_COPIES = 128
MESH = pl.DeviceIdType.MESH
F32, BF16 = jnp.float32, jnp.bfloat16


def dot(a, b, over_a, over_b):
    return lax.dot_general(a, b, (((over_a,), (over_b,)), ((), ())), preferred_element_type=F32)


def groups_of(width, depth):
    half, tiles = width // 2, depth // LANES
    cut = tiles * 2 // 3
    groups = []
    for first, last, order in ((0, cut, "xyz"), (cut, tiles, "yxz")):
        counts = [{"x": NX, "y": NY, "z": NZ}[axis] for axis in order]
        held = [(last - first) * half]
        for count in counts:
            held.append(-(-held[-1] // (count * ROW_TILE)) * ROW_TILE)
        groups.append((first, last, order, counts, held))
    return groups


class Copies:
    def __init__(self, send_sem, recv_sem):
        self.send_sem, self.recv_sem, self.made = send_sem, recv_sem, []

    def start(self, source, target, device):
        i = len(self.made)
        copy = remote(source, target, self.send_sem.at[i], self.recv_sem.at[i], device)
        copy.start()
        self.made.append(copy)
        return copy


def remote(source, target, send_sem, recv_sem, device):
    return pltpu.make_async_remote_copy(
        src_ref=source,
        dst_ref=target,
        send_sem=send_sem,
        recv_sem=recv_sem,
        device_id=device,
        device_id_type=MESH,
    )


def rows_of(ref, place, count):
    return ref.at[pl.ds(pl.multiple_of(place * count, ROW_TILE), count)]


def kernel(
    x_hbm,
    w_hbm,
    t_hbm,
    matched_ref,
    scale_ref,
    offset_ref,
    loss_ref,
    grad_ref,
    cap_ref,
    x_all,
    w_ref,
    text_raw,
    text_low,
    image_unit,
    image_low,
    sums_out,
    sums_in,
    text_sums,
    cos_out,
    cos_in,
    weight,
    back,
    back_all,
    loss_core,
    loss_x,
    loss_y,
    loss_z,
    text_dir,
    text_part,
    presum_in,
    presum_out,
    text_in,
    tdot_out,
    tdot_in,
    *rest,
):
    *buffers, load_sem, text_send, text_recv, cos_send, cos_recv, part_send, part_recv, send_sem, recv_sem = rest
    width, rows = t_hbm.shape
    depth = x_hbm.shape[1]
    half, hr = width // 2, rows // 2
    dp, mp = lax.axis_index("dp"), lax.axis_index("mp")
    core = lax.rem(dp, 2)
    at = {"x": lax.rem(dp // 2, NX), "y": lax.rem(dp // (2 * NX), NY), "z": dp // (2 * NX * NY)}
    counts = {"x": NX, "y": NY, "z": NZ}
    strides = {"x": 2, "y": 2 * NX, "z": 2 * NX * NY}
    other_mp = (dp, 1 - mp)
    other_core = (dp + 1 - 2 * core, mp)

    def along_dp(step):
        return (lax.rem(dp + step + BLOCKS, BLOCKS), mp)

    def others(axis):
        places = [lax.rem(at[axis] + k, counts[axis]) for k in range(1, counts[axis])]
        return [(place, (dp + (place - at[axis]) * strides[axis], mp)) for place in places]

    def source_of(axis, k):
        return lax.rem(at[axis] - k + counts[axis], counts[axis])

    halves = [t_hbm.at[:, :hr], t_hbm.at[:, hr:]]
    loads = [
        pltpu.make_async_copy(halves[0], text_raw.at[0, 0], load_sem.at[0]),
        pltpu.make_async_copy(halves[1], text_raw.at[0, 1], load_sem.at[1]),
        pltpu.make_async_copy(w_hbm, w_ref, load_sem.at[2]),
        pltpu.make_async_copy(x_hbm, x_all.at[core], load_sem.at[3]),
    ]
    for load in loads:
        load.start()

    barrier = pltpu.get_barrier_semaphore()
    greeted = [other_mp, other_core] + [along_dp(s) for s in (-2, -1, 1, 2)]
    greeted += [device for axis in "xyz" for _, device in others(axis)]
    for device in greeted:
        pl.semaphore_signal(barrier, inc=1, device_id=device, device_id_type=MESH)
    pl.semaphore_wait(barrier, len(greeted))

    copies = Copies(send_sem, recv_sem)
    send = copies.start

    def text_copy(h, step, number):
        return remote(
            halves[h],
            text_raw.at[step, h],
            text_send.at[number],
            text_recv.at[step - 1, h],
            along_dp(step),
        )

    both = [text_copy(0, 1, 0), text_copy(1, 2, 1)]
    first_only = [text_copy(0, 2, 2), text_copy(1, 1, 3)]
    for copy in both:
        copy.start()

    @pl.when(core == 0)
    def _():
        for copy in first_only:
            copy.start()

    def text_arrived(step, h):
        remote(halves[0], text_raw.at[step, h], text_send.at[4], text_recv.at[step - 1, h], other_core).wait_recv()

    relay = remote(
        text_raw.at[1 + core, core],
        text_raw.at[2 - core, core],
        text_send.at[4],
        text_recv.at[1 - core, core],
        other_core,
    )

    for load in loads:
        load.wait()
    x_there = send(x_all.at[core], x_all.at[core], other_core)
    image_raw = dot(w_ref[...], x_all[core], 1, 1)
    sums_out[0:1, :] = jnp.sum(image_raw * image_raw, axis=0, keepdims=True)
    for h in (0, 1):
        own_text = text_raw[0, h].astype(F32)
        sums_out[1:2, h * hr : (h + 1) * hr] = jnp.sum(own_text * own_text, axis=0, keepdims=True)
    sums_there = send(sums_out, sums_in, other_mp)
    sums_there.wait_recv()
    sums = sums_out[...] + sums_in[...]
    image_scale = lax.rsqrt(sums[0:1, :] + EPSILON)
    text_scale = lax.rsqrt(sums[1:2, :] + EPSILON)
    text_sums[0] = sums
    text_sums_there = [send(text_sums.at[0], text_sums.at[s], along_dp(s)) for s in (1, 2)]
    unit = image_raw * image_scale
    image_unit[...] = unit
    image_low[...] = unit.astype(BF16)

    def cos_copy(s, h):
        return remote(cos_out.at[s, h], cos_in.at[s, h], cos_send.at[s, h], cos_recv.at[s, h], other_mp)

    def cosines(s, h):
        scale = lax.rsqrt(text_sums[s, 1:2, :] + EPSILON)
        if isinstance(h, int):
            scale = scale[:, h * hr : (h + 1) * hr]
        else:
            scale = jnp.where(h == 0, scale[:, :hr], scale[:, hr:])
        low = (text_raw[s, h].astype(F32) * scale).astype(BF16)
        text_low[s, h] = low
        cos_out[s, h] = dot(low, image_low[...], 0, 0).astype(BF16)
        cos_copy(s, h).start()

    cosines(0, 0)
    cosines(0, 1)
    for copy in text_sums_there:
        copy.wait_recv()
    units = [(1, 0), (2 - core, core), (2, 1), (1 + core, 1 - core)]
    for number, (s, h) in enumerate(units):
        text_arrived(s, h)
        if number in (0, 2):

            @pl.when(core == number // 2)
            def _():
                relay.start()

        cosines(s, h)

    sharpness, offset = scale_ref[0], offset_ref[0]
    loss_rows = jnp.zeros((1, rows), F32)
    along_unit = jnp.zeros((1, rows), F32)
    direction = jnp.zeros((width, rows), F32)
    for s, h in [(0, 0), (0, 1)] + units:
        cos_copy(s, h).wait_recv()
        cos = cos_out[s, h].astype(F32) + cos_in[s, h].astype(F32)
        first = lax.rem(dp - s + BLOCKS, BLOCKS) * rows + h * hr
        matched = first + lax.broadcasted_iota(jnp.int32, (hr, rows), 0) == matched_ref[...]
        logit = sharpness * cos + offset
        against = jnp.where(matched, -logit, logit)
        small = jnp.exp(-jnp.abs(against))
        loss_rows += jnp.sum(jnp.maximum(against, 0.0) + jnp.log1p(small), axis=0, keepdims=True)
        sigmoid = jnp.where(against >= 0.0, 1.0, small) / (1.0 + small)
        low = (jnp.where(matched, -sigmoid, sigmoid) * sharpness).astype(BF16)
        weight[s, h] = low
        along_unit += jnp.sum(low.astype(F32) * cos, axis=0, keepdims=True)
        direction += dot(text_low[s, h], low, 1, 0)

    image_back = ((direction - image_unit[...] * along_unit) * image_scale).astype(BF16)
    back[0] = image_back[:half]
    back[1] = image_back[half:]
    back_there = send(back.at[1 - core], back_all.at[core], other_core)
    back_all[core] = back[core]
    loss_core[core] = jnp.broadcast_to(loss_rows, (8, rows))
    loss_core_there = send(loss_core.at[core], loss_core.at[core], other_core)

    def text_parts(s, h):
        text_part[s - 1, h] = dot(image_low[...], weight[s, h], 1, 1).astype(BF16)

    shared, alone = 1 + core, 2 - core
    text_parts(shared, 1 - core)
    presum_there = send(text_part.at[core, 1 - core], presum_in, other_core)

    def part_copy(source, which, h, step, number):
        return remote(
            source, text_in.at[which, h], part_send.at[number], part_recv.at[which, h], along_dp(-step)
        )

    part_copies = []
    for h in (0, 1):
        text_parts(alone, h)
        part_copies.append(part_copy(text_part.at[1 - core, h], 1 - core, h, alone, h))
        part_copies[-1].start()

    x_there.wait_recv()
    back_there.wait_recv()
    mine, theirs = back_all[core], back_all[1 - core]
    x_mine, x_theirs = x_all[core], x_all[1 - core]
    groups = groups_of(width, depth)
    levels = []
    for g, (first, last, order, _, held) in enumerate(groups):
        full, sums_2, sums_3, land_1, land_2, land_3, got_3, got_2, result = buffers[9 * g : 9 * g + 9]
        levels.append(([full, sums_2, sums_3], [land_1, land_2, land_3], [result, got_2, got_3]))

    def scatter(g, level):
        _, _, order, _, held = groups[g]
        source, landing = levels[g][0][level], levels[g][1][level]
        return [
            send(rows_of(source, place, held[level + 1]), landing.at[k], device)
            for k, (place, device) in enumerate(others(order[level]))
        ]

    def scattered(g, level, there):
        _, _, order, _, held = groups[g]
        source, landing = levels[g][0][level], levels[g][1][level]
        total = rows_of(source, at[order[level]], held[level + 1])[...].astype(F32)
        for k, copy in enumerate(there):
            copy.wait_recv()
            total += landing[k].astype(F32)
        return total.astype(BF16)

    def padded(ref, count):
        if ref.shape[0] > count:
            ref[count:, :] = jnp.zeros((ref.shape[0] - count, LANES), BF16)

    def loss_spread(landing, axis, value):
        landing[at[axis]] = value
        return [send(landing.at[at[axis]], landing.at[at[axis]], device) for _, device in others(axis)]

    def loss_sum(there, landing, axis):
        for copy in there:
            copy.wait_recv()
        total = landing[0]
        for k in range(1, counts[axis]):
            total += landing[k]
        return total

    there = []
    for g, (first, last, order, _, held) in enumerate(groups):
        full = levels[g][0][0]
        for k in range(first, last):
            cols = slice(k * LANES, (k + 1) * LANES)
            part = dot(mine, x_mine[:, cols], 1, 0) + dot(theirs, x_theirs[:, cols], 1, 0)
            full[(k - first) * half : (k - first + 1) * half, :] = part.astype(BF16)
        padded(full, held[0])
        there.append(scatter(g, 0))
    loss_core_there.wait_recv()
    loss_there = loss_spread(loss_x, "x", loss_core[0] + loss_core[1])

    text_parts(shared, core)
    for h in (0, 1):
        text_dir[h] = dot(image_low[...], weight[0, h], 1, 1)
    presum_there.wait_recv()
    presum_out[...] = (text_part[core, core].astype(F32) + presum_in[...].astype(F32)).astype(BF16)
    part_copies.append(part_copy(presum_out, 0, core, shared, 2))
    part_copies[-1].start()

    for level in range(3):
        for g, (_, _, order, _, held) in enumerate(groups):
            total = scattered(g, level, there[g])
            if level < 2:
                target = levels[g][0][level + 1]
                target[: held[level + 1], :] = total
                padded(target, held[level + 1])
                there[g] = scatter(g, level + 1)
            else:
                own = rows_of(levels[g][2][2], at[order[2]], held[3])
                own[...] = total
                there[g] = [send(own, own, device) for _, device in others(order[2])]
        if level == 0:
            loss_there = loss_spread(loss_y, "y", loss_sum(loss_there, loss_x, "x"))
        if level == 1:
            loss_there = loss_spread(loss_z, "z", loss_sum(loss_there, loss_y, "y"))

    loss_now = loss_sum(loss_there, loss_z, "z")
    loss_ref[0] = jnp.sum(loss_now[0:1, :]) / (rows * BLOCKS)

    def part_arrived(which, h):
        part_copy(presum_out, which, h, 1, 2).wait_recv()

    for h in (0, 1):
        part_arrived(0, h)
        text_dir[h] += text_in[0, h].astype(F32)

    @pl.when(core == 0)
    def _():
        for h in (0, 1):
            part_arrived(1, h)
            text_dir[h] += text_in[1, h].astype(F32)

    def text_unit(h):
        return text_raw[0, h].astype(F32) * text_scale[:, h * hr : (h + 1) * hr]

    for h in (0, 1):
        tdot_out[:, h * hr : (h + 1) * hr] = jnp.broadcast_to(
            jnp.sum(text_unit(h) * text_dir[h], axis=0, keepdims=True), (8, hr)
        )
    tdot_there = send(tdot_out, tdot_in, other_mp)

    for g, (_, _, order, _, held) in enumerate(groups):
        for copy in there[g]:
            copy.wait_recv()
        own = rows_of(levels[g][2][1], at[order[1]], held[2])
        own[...] = levels[g][2][2][: held[2], :]
        there[g] = [send(own, own, device) for _, device in others(order[1])]

    tdot_there.wait_recv()
    tdot = tdot_out[0:1, :] + tdot_in[0:1, :]
    for h in (0, 1):
        lanes = slice(h * hr, (h + 1) * hr)
        cap_ref[:, lanes] = (
            (text_dir[h] - text_unit(h) * tdot[:, lanes]) * text_scale[:, lanes]
        ).astype(BF16)

    def chunk(g, place):
        return rows_of(levels[g][2][0].at[core], place, groups[g][4][1])

    relayed = []
    for g, (_, _, order, _, held) in enumerate(groups):
        for copy in there[g]:
            copy.wait_recv()
        own = chunk(g, at[order[0]])
        own[...] = levels[g][2][1][: held[1], :]
        there[g] = [send(own, own, device) for _, device in others(order[0])]
        relayed.append(send(own, own, other_core))
    for g, (_, _, order, _, held) in enumerate(groups):
        for k, copy in enumerate(there[g]):
            copy.wait_recv()
            arrived = chunk(g, source_of(order[0], k + 1))
            relayed.append(send(arrived, arrived, other_core))
    for copy in relayed:
        copy.wait_recv()
    for g, (first, last, _, _, _) in enumerate(groups):
        result = levels[g][2][0]
        for c in range(2):
            for k in range(first, last):
                rows_k = slice((k - first) * half, (k - first + 1) * half)
                grad_ref[c * half : (c + 1) * half, k * LANES : (k + 1) * LANES] = result[c, rows_k, :]

    for copy in copies.made + both + [relay] + part_copies:
        copy.wait_send()

    @pl.when(core == 0)
    def _():
        for copy in first_only:
            copy.wait_send()

    for s in range(STEPS + 1):
        for h in (0, 1):
            cos_copy(s, h).wait_send()


def local(x_rows, w_half, t_half, matched, sharpness, offset):
    rows, depth = x_rows.shape
    width = w_half.shape[1]
    half, hr = width // 2, rows // 2
    vmem, hbm = pl.BlockSpec(memory_space=pltpu.VMEM), pl.BlockSpec(memory_space=pltpu.HBM)
    smem = pl.BlockSpec(memory_space=pltpu.SMEM)
    buffers = []
    for _, _, _, (n1, n2, n3), (_, r1, r2, r3) in groups_of(width, depth):
        buffers += [
            pltpu.VMEM((n1 * r1, LANES), BF16),
            pltpu.VMEM((n2 * r2, LANES), BF16),
            pltpu.VMEM((n3 * r3, LANES), BF16),
            pltpu.VMEM((n1 - 1, r1, LANES), BF16),
            pltpu.VMEM((n2 - 1, r2, LANES), BF16),
            pltpu.VMEM((n3 - 1, r3, LANES), BF16),
            pltpu.VMEM((n3 * r3, LANES), BF16),
            pltpu.VMEM((n2 * r2, LANES), BF16),
            pltpu.VMEM((2, n1 * r1, LANES), BF16),
        ]
    call = pl.pallas_call(
        kernel,
        out_shape=(
            jax.ShapeDtypeStruct((1,), F32),
            jax.ShapeDtypeStruct((width, depth), BF16),
            jax.ShapeDtypeStruct((width, rows), BF16),
        ),
        in_specs=[hbm, hbm, hbm, vmem, smem, smem],
        out_specs=(smem, vmem, vmem),
        scratch_shapes=[
            pltpu.VMEM((2, rows, depth), BF16),
            pltpu.VMEM((width, depth), BF16),
            pltpu.VMEM((3, 2, width, hr), BF16),
            pltpu.VMEM((3, 2, width, hr), BF16),
            pltpu.VMEM((width, rows), F32),
            pltpu.VMEM((width, rows), BF16),
            pltpu.VMEM((8, rows), F32),
            pltpu.VMEM((8, rows), F32),
            pltpu.VMEM((3, 8, rows), F32),
            pltpu.VMEM((3, 2, hr, rows), BF16),
            pltpu.VMEM((3, 2, hr, rows), BF16),
            pltpu.VMEM((3, 2, hr, rows), BF16),
            pltpu.VMEM((2, half, rows), BF16),
            pltpu.VMEM((2, half, rows), BF16),
            pltpu.VMEM((2, 8, rows), F32),
            pltpu.VMEM((NX, 8, rows), F32),
            pltpu.VMEM((NY, 8, rows), F32),
            pltpu.VMEM((NZ, 8, rows), F32),
            pltpu.VMEM((2, width, hr), F32),
            pltpu.VMEM((2, 2, width, hr), BF16),
            pltpu.VMEM((width, hr), BF16),
            pltpu.VMEM((width, hr), BF16),
            pltpu.VMEM((2, 2, width, hr), BF16),
            pltpu.VMEM((8, rows), F32),
            pltpu.VMEM((8, rows), F32),
            *buffers,
            pltpu.SemaphoreType.DMA((4,)),
            pltpu.SemaphoreType.DMA((5,)),
            pltpu.SemaphoreType.DMA((2, 2)),
            pltpu.SemaphoreType.DMA((3, 2)),
            pltpu.SemaphoreType.DMA((3, 2)),
            pltpu.SemaphoreType.DMA((3,)),
            pltpu.SemaphoreType.DMA((2, 2)),
            pltpu.SemaphoreType.DMA((N_COPIES,)),
            pltpu.SemaphoreType.DMA((N_COPIES,)),
        ],
        compiler_params=pltpu.CompilerParams(
            collective_id=0, has_side_effects=True, vmem_limit_bytes=40 * 1024 * 1024
        ),
    )
    loss, grad, cap = call(x_rows, w_half.T, t_half.T, matched.reshape(1, rows), sharpness, offset)
    return (loss, grad.T, cap.T)


def solution(mesh):
    placed = (P("dp", None), P(None, "mp"), P("dp", "mp"), P("dp"), P(), P())
    return jax.shard_map(
        local,
        mesh=mesh,
        in_specs=placed,
        out_specs=(P(), P(None, "mp"), P("dp", "mp")),
        check_vma=False,
    )
```

```python
import jax
import jax.numpy as jnp
from jax import lax
from jax.experimental import pallas as pl
from jax.experimental.pallas import tpu as pltpu
from jax.sharding import PartitionSpec as P

STEPS = 2
NX, NY, NZ = 4, 8, 4
BLOCKS = NX * NY * NZ * 2
EPSILON = 1e-06
ROW_TILE = 16
LANES = 128
N_COPIES = 128
MESH = pl.DeviceIdType.MESH
F32, BF16 = jnp.float32, jnp.bfloat16


def dot(a, b, over_a, over_b):
    return lax.dot_general(a, b, (((over_a,), (over_b,)), ((), ())), preferred_element_type=F32)


def groups_of(width, depth):
    half, tiles = width // 2, depth // LANES
    one, two = tiles * 6 // 9, tiles * 7 // 9
    groups = []
    for first, last, order in ((0, one, "xyz"), (one, two, "yxz"), (two, tiles, "zxy")):
        counts = [{"x": NX, "y": NY, "z": NZ}[axis] for axis in order]
        held = [(last - first) * half]
        for count in counts[:2]:
            held.append(-(-held[-1] // (count * ROW_TILE)) * ROW_TILE)
        groups.append((first, last, order, counts, held))
    return groups


class Copies:
    def __init__(self, send_sem, recv_sem):
        self.send_sem, self.recv_sem, self.made = send_sem, recv_sem, []

    def start(self, source, target, device):
        i = len(self.made)
        copy = remote(source, target, self.send_sem.at[i], self.recv_sem.at[i], device)
        copy.start()
        self.made.append(copy)
        return copy


def remote(source, target, send_sem, recv_sem, device):
    return pltpu.make_async_remote_copy(
        src_ref=source,
        dst_ref=target,
        send_sem=send_sem,
        recv_sem=recv_sem,
        device_id=device,
        device_id_type=MESH,
    )


def rows_of(ref, place, count):
    return ref.at[pl.ds(pl.multiple_of(place * count, ROW_TILE), count)]


def kernel(
    x_hbm,
    w_hbm,
    t_hbm,
    matched_ref,
    scale_ref,
    offset_ref,
    loss_ref,
    grad_ref,
    cap_ref,
    x_all,
    w_ref,
    text_raw,
    text_low,
    image_unit,
    image_low,
    sums_out,
    sums_in,
    text_sums,
    cos_out,
    cos_in,
    weight,
    back,
    back_all,
    loss_core,
    loss_x,
    loss_y,
    loss_z,
    text_dir,
    text_part,
    presum_in,
    presum_out,
    text_in,
    tdot_out,
    tdot_in,
    *rest,
):
    *buffers, grad_own, passed, passed_send, passed_recv, load_sem, text_send, text_recv, cos_send, cos_recv, part_send, part_recv, send_sem, recv_sem = rest
    width, rows = t_hbm.shape
    depth = x_hbm.shape[1]
    half, hr = width // 2, rows // 2
    dp, mp = lax.axis_index("dp"), lax.axis_index("mp")
    core = lax.rem(dp, 2)
    at = {"x": lax.rem(dp // 2, NX), "y": lax.rem(dp // (2 * NX), NY), "z": dp // (2 * NX * NY)}
    counts = {"x": NX, "y": NY, "z": NZ}
    strides = {"x": 2, "y": 2 * NX, "z": 2 * NX * NY}
    other_mp = (dp, 1 - mp)
    other_core = (dp + 1 - 2 * core, mp)

    def along_dp(step):
        return (lax.rem(dp + step + 2 * BLOCKS, BLOCKS), mp)

    def others(axis):
        places = [lax.rem(at[axis] + k, counts[axis]) for k in range(1, counts[axis])]
        return [(place, (dp + (place - at[axis]) * strides[axis], mp)) for place in places]

    def source_of(axis, k):
        return lax.rem(at[axis] - k + counts[axis], counts[axis])

    halves = [text_raw.at[0, 0], text_raw.at[0, 1]]
    loads = [
        pltpu.make_async_copy(t_hbm.at[:, :hr], text_raw.at[0, 0], load_sem.at[0]),
        pltpu.make_async_copy(t_hbm.at[:, hr:], text_raw.at[0, 1], load_sem.at[1]),
        pltpu.make_async_copy(w_hbm, w_ref, load_sem.at[2]),
        pltpu.make_async_copy(x_hbm, x_all.at[core], load_sem.at[3]),
    ]
    for load in loads:
        load.start()

    barrier = pltpu.get_barrier_semaphore()
    greeted = [other_mp, other_core] + [along_dp(s) for s in (-2, -1, 1, 2)]
    greeted += [device for axis in "xyz" for _, device in others(axis)]
    for device in greeted:
        pl.semaphore_signal(barrier, inc=1, device_id=device, device_id_type=MESH)

    chip, plane = 2 * NX, 2 * NX * NY
    corner = (at["x"] == NX - 1) & (at["y"] == NY - 1)
    landing = (at["x"] == 0) & (at["y"] == 0)
    via_z = corner & (core == 1)
    via_x = (at["x"] == 0) & (at["y"] == NY - 1) & (core == 0)
    via_y = (at["x"] == NX - 1) & (at["y"] == 1) & (core == 0)
    passes_on = via_z | via_x | via_y
    back_z, back_x, back_y = -plane, 2 * (NX - 1), (NY - 2) * chip - plane
    back_here = jnp.where(via_z, back_z, jnp.where(via_x, back_x, back_y))

    def greet(device):
        pl.semaphore_signal(barrier, inc=1, device_id=device, device_id_type=MESH)

    @pl.when(passes_on)
    def _():
        greet(along_dp(back_here))

    @pl.when(landing & (core == 0))
    def _():
        greet(along_dp(-2 - back_x))
        greet(along_dp(-2 - back_y))

    @pl.when(landing & (core == 1))
    def _():
        greet(along_dp(-2 - back_z))

    more = jnp.where(passes_on, 1, 0) + jnp.where(corner, 2 - core, 0)
    for load in loads[:2]:
        load.wait()
    pl.semaphore_wait(barrier, len(greeted) + more)

    copies = Copies(send_sem, recv_sem)
    send = copies.start

    def text_copy(h, step, number):
        return remote(
            halves[h],
            text_raw.at[step, h],
            text_send.at[number],
            text_recv.at[step - 1, h],
            along_dp(step),
        )

    def text_away(h, back, number):
        return remote(halves[h], passed, text_send.at[number], passed_recv.at[0], along_dp(-back))

    straight = ~corner

    @pl.when((core == 1) | straight)
    def _():
        text_copy(0, 1, 0).start()

    @pl.when(straight)
    def _():
        text_copy(1, 2, 1).start()

    @pl.when((core == 0) & straight)
    def _():
        text_copy(0, 2, 2).start()
        text_copy(1, 1, 3).start()

    @pl.when((core == 1) & corner)
    def _():
        text_away(1, back_z, 1).start()

    @pl.when((core == 0) & corner)
    def _():
        text_away(0, back_x, 2).start()
        text_away(1, back_y, 1).start()
        text_copy(0, 1, 0).start()
        text_copy(1, 1, 3).start()

    pass_half = jnp.where(via_x, 0, 1)
    pass_on = remote(
        passed,
        text_raw.at[2, pass_half],
        passed_send.at[0],
        text_recv.at[1, pass_half],
        along_dp(back_here + 2),
    )

    def text_arrived(step, h):
        remote(halves[0], text_raw.at[step, h], text_send.at[4], text_recv.at[step - 1, h], other_core).wait_recv()

    relay = remote(
        text_raw.at[1 + core, core],
        text_raw.at[2 - core, core],
        text_send.at[4],
        text_recv.at[1 - core, core],
        other_core,
    )

    for load in loads[2:]:
        load.wait()
    x_there = send(x_all.at[core], x_all.at[core], other_core)
    image_raw = dot(w_ref[...], x_all[core], 1, 1)
    sums_out[0:1, :] = jnp.sum(image_raw * image_raw, axis=0, keepdims=True)
    for h in (0, 1):
        own_text = text_raw[0, h].astype(F32)
        sums_out[1:2, h * hr : (h + 1) * hr] = jnp.sum(own_text * own_text, axis=0, keepdims=True)
    sums_there = send(sums_out, sums_in, other_mp)

    @pl.when(passes_on)
    def _():
        remote(halves[0], passed, passed_send.at[0], passed_recv.at[0], other_core).wait_recv()
        pass_on.start()

    sums_there.wait_recv()
    sums = sums_out[...] + sums_in[...]
    image_scale = lax.rsqrt(sums[0:1, :] + EPSILON)
    text_scale = lax.rsqrt(sums[1:2, :] + EPSILON)
    text_sums[0] = sums
    text_sums_there = [send(text_sums.at[0], text_sums.at[s], along_dp(s)) for s in (1, 2)]
    unit = image_raw * image_scale
    image_unit[...] = unit
    image_low[...] = unit.astype(BF16)

    def cos_copy(s, h):
        return remote(cos_out.at[s, h], cos_in.at[s, h], cos_send.at[s, h], cos_recv.at[s, h], other_mp)

    def cosines(s, h):
        scale = lax.rsqrt(text_sums[s, 1:2, :] + EPSILON)
        if isinstance(h, int):
            scale = scale[:, h * hr : (h + 1) * hr]
        else:
            scale = jnp.where(h == 0, scale[:, :hr], scale[:, hr:])
        low = (text_raw[s, h].astype(F32) * scale).astype(BF16)
        text_low[s, h] = low
        cos_out[s, h] = dot(low, image_low[...], 0, 0).astype(BF16)
        cos_copy(s, h).start()

    cosines(0, 0)
    cosines(0, 1)
    for copy in text_sums_there:
        copy.wait_recv()
    units = [(1, 0), (2 - core, core), (2, 1), (1 + core, 1 - core)]
    for number, (s, h) in enumerate(units):
        text_arrived(s, h)
        if number in (0, 2):

            @pl.when(core == number // 2)
            def _():
                relay.start()

        cosines(s, h)

    sharpness, offset = scale_ref[0], offset_ref[0]
    loss_rows = jnp.zeros((1, rows), F32)
    along_unit = jnp.zeros((1, rows), F32)
    direction = jnp.zeros((width, rows), F32)
    for s, h in [(0, 0), (0, 1)] + units:
        cos_copy(s, h).wait_recv()
        cos = cos_out[s, h].astype(F32) + cos_in[s, h].astype(F32)
        first = lax.rem(dp - s + BLOCKS, BLOCKS) * rows + h * hr
        matched = first + lax.broadcasted_iota(jnp.int32, (hr, rows), 0) == matched_ref[...]
        logit = sharpness * cos + offset
        against = jnp.where(matched, -logit, logit)
        small = jnp.exp(-jnp.abs(against))
        loss_rows += jnp.sum(jnp.maximum(against, 0.0) + jnp.log1p(small), axis=0, keepdims=True)
        sigmoid = jnp.where(against >= 0.0, 1.0, small) / (1.0 + small)
        low = (jnp.where(matched, -sigmoid, sigmoid) * sharpness).astype(BF16)
        weight[s, h] = low
        along_unit += jnp.sum(low.astype(F32) * cos, axis=0, keepdims=True)
        direction += dot(text_low[s, h], low, 1, 0)

    image_back = ((direction - image_unit[...] * along_unit) * image_scale).astype(BF16)
    back[0] = image_back[:half]
    back[1] = image_back[half:]
    back_there = send(back.at[1 - core], back_all.at[core], other_core)
    back_all[core] = back[core]
    loss_core[core] = jnp.broadcast_to(loss_rows, (8, rows))
    loss_core_there = send(loss_core.at[core], loss_core.at[core], other_core)

    def text_parts(s, h):
        text_part[s - 1, h] = dot(image_low[...], weight[s, h], 1, 1).astype(BF16)

    shared, alone = 1 + core, 2 - core
    def part_copy(source, which, h, step, number):
        return remote(
            source, text_in.at[which, h], part_send.at[number], part_recv.at[which, h], along_dp(-step)
        )

    grad_own[...] = dot(back_all[core], x_all[core], 1, 0)
    x_there.wait_recv()
    back_there.wait_recv()
    theirs, x_theirs = back_all[1 - core], x_all[1 - core]
    groups = groups_of(width, depth)
    levels = []
    for g, (first, last, order, _, held) in enumerate(groups):
        full, sums_2, land_1, land_2, land_3, got_2, result = buffers[7 * g : 7 * g + 7]
        levels.append(([full, sums_2], [land_1, land_2, land_3], [result, got_2]))

    def scatter(g, level):
        _, _, order, _, held = groups[g]
        source, landing = levels[g][0][level], levels[g][1][level]
        return [
            send(rows_of(source, place, held[level + 1]), landing.at[k], device)
            for k, (place, device) in enumerate(others(order[level]))
        ]

    def scattered(g, level, there):
        _, _, order, _, held = groups[g]
        source, landing = levels[g][0][level], levels[g][1][level]
        total = rows_of(source, at[order[level]], held[level + 1])[...].astype(F32)
        for k, copy in enumerate(there):
            copy.wait_recv()
            total += landing[k].astype(F32)
        return total.astype(BF16)

    def padded(ref, count):
        if ref.shape[0] > count:
            ref[count:, :] = jnp.zeros((ref.shape[0] - count, LANES), BF16)

    def spread(landing, axis, value):
        landing[at[axis]] = value
        return [send(landing.at[at[axis]], landing.at[at[axis]], device) for _, device in others(axis)]

    def loss_sum(there, landing, axis):
        for copy in there:
            copy.wait_recv()
        total = landing[0]
        for k in range(1, counts[axis]):
            total += landing[k]
        return total

    there = []
    for g, (first, last, order, _, held) in enumerate(groups):
        full = levels[g][0][0]
        for k in range(first, last):
            cols = slice(k * LANES, (k + 1) * LANES)
            part = grad_own[:, cols] + dot(theirs, x_theirs[:, cols], 1, 0)
            full[(k - first) * half : (k - first + 1) * half, :] = part.astype(BF16)
        padded(full, held[0])
        there.append(scatter(g, 0))
    loss_core_there.wait_recv()
    loss_there = spread(loss_x, "x", loss_core[0] + loss_core[1])

    text_parts(shared, 1 - core)
    presum_there = send(text_part.at[core, 1 - core], presum_in, other_core)
    text_parts(shared, core)
    for h in (0, 1):
        text_parts(alone, h)
    for h in (0, 1):
        text_dir[h] = dot(image_low[...], weight[0, h], 1, 1)
    presum_there.wait_recv()
    presum_out[...] = (text_part[core, core].astype(F32) + presum_in[...].astype(F32)).astype(BF16)
    part_copies = [
        part_copy(text_part.at[1 - core, h], 1 - core, h, alone, h) for h in (0, 1)
    ] + [part_copy(presum_out, 0, core, shared, 2)]

    for g, (_, _, order, _, held) in enumerate(groups):
        target = levels[g][0][1]
        target[: held[1], :] = scattered(g, 0, there[g])
        padded(target, held[1])
        there[g] = scatter(g, 1)
    loss_there = spread(loss_y, "y", loss_sum(loss_there, loss_x, "x"))
    for copy in part_copies:
        copy.start()
    for g, (_, _, order, _, held) in enumerate(groups):
        there[g] = spread(levels[g][1][2], order[2], scattered(g, 1, there[g]))
    loss_there = spread(loss_z, "z", loss_sum(loss_there, loss_y, "y"))
    for g, (_, _, order, counts_g, held) in enumerate(groups):
        landing_g = levels[g][1][2]
        for copy in there[g]:
            copy.wait_recv()
        total = landing_g[0].astype(F32)
        for k in range(1, counts_g[2]):
            total += landing_g[k].astype(F32)
        own = rows_of(levels[g][2][1], at[order[1]], held[2])
        own[...] = total.astype(BF16)
        there[g] = [send(own, own, device) for _, device in others(order[1])]

    loss_now = loss_sum(loss_there, loss_z, "z")
    loss_ref[0] = jnp.sum(loss_now[0:1, :]) / (rows * BLOCKS)

    def part_arrived(which, h):
        part_copy(presum_out, which, h, 1, 2).wait_recv()

    for h in (0, 1):
        part_arrived(0, h)
        text_dir[h] += text_in[0, h].astype(F32)

    @pl.when(core == 0)
    def _():
        for h in (0, 1):
            part_arrived(1, h)
            text_dir[h] += text_in[1, h].astype(F32)

    def text_unit(h):
        return text_raw[0, h].astype(F32) * text_scale[:, h * hr : (h + 1) * hr]

    for h in (0, 1):
        tdot_out[:, h * hr : (h + 1) * hr] = jnp.broadcast_to(
            jnp.sum(text_unit(h) * text_dir[h], axis=0, keepdims=True), (8, hr)
        )
    tdot_there = send(tdot_out, tdot_in, other_mp)

    tdot_there.wait_recv()
    tdot = tdot_out[0:1, :] + tdot_in[0:1, :]
    for h in (0, 1):
        lanes = slice(h * hr, (h + 1) * hr)
        cap_ref[:, lanes] = (
            (text_dir[h] - text_unit(h) * tdot[:, lanes]) * text_scale[:, lanes]
        ).astype(BF16)

    def chunk(g, place):
        return rows_of(levels[g][2][0].at[core], place, groups[g][4][1])

    relayed = []
    for g, (_, _, order, _, held) in enumerate(groups):
        for copy in there[g]:
            copy.wait_recv()
        own = chunk(g, at[order[0]])
        own[...] = levels[g][2][1][: held[1], :]
        there[g] = [send(own, own, device) for _, device in others(order[0])]
        relayed.append(send(own, own, other_core))
    for g, (_, _, order, _, held) in enumerate(groups):
        for k, copy in enumerate(there[g]):
            copy.wait_recv()
            arrived = chunk(g, source_of(order[0], k + 1))
            relayed.append(send(arrived, arrived, other_core))
    for copy in relayed:
        copy.wait_recv()
    for g, (first, last, _, _, _) in enumerate(groups):
        result = levels[g][2][0]
        for c in range(2):
            for k in range(first, last):
                rows_k = slice((k - first) * half, (k - first + 1) * half)
                grad_ref[c * half : (c + 1) * half, k * LANES : (k + 1) * LANES] = result[c, rows_k, :]

    for copy in copies.made + [text_copy(0, 1, 0), text_copy(1, 2, 1), relay] + part_copies:
        copy.wait_send()

    @pl.when(core == 0)
    def _():
        for copy in (text_copy(0, 2, 2), text_copy(1, 1, 3)):
            copy.wait_send()

    @pl.when(passes_on)
    def _():
        pass_on.wait_send()

    for s in range(STEPS + 1):
        for h in (0, 1):
            cos_copy(s, h).wait_send()


def local(x_rows, w_half, t_half, matched, sharpness, offset):
    rows, depth = x_rows.shape
    width = w_half.shape[1]
    half, hr = width // 2, rows // 2
    vmem, hbm = pl.BlockSpec(memory_space=pltpu.VMEM), pl.BlockSpec(memory_space=pltpu.HBM)
    smem = pl.BlockSpec(memory_space=pltpu.SMEM)
    buffers = []
    for _, _, _, (n1, n2, n3), (_, r1, r2) in groups_of(width, depth):
        buffers += [
            pltpu.VMEM((n1 * r1, LANES), BF16),
            pltpu.VMEM((n2 * r2, LANES), BF16),
            pltpu.VMEM((n1 - 1, r1, LANES), BF16),
            pltpu.VMEM((n2 - 1, r2, LANES), BF16),
            pltpu.VMEM((n3, r2, LANES), BF16),
            pltpu.VMEM((n2 * r2, LANES), BF16),
            pltpu.VMEM((2, n1 * r1, LANES), BF16),
        ]
    call = pl.pallas_call(
        kernel,
        out_shape=(
            jax.ShapeDtypeStruct((1,), F32),
            jax.ShapeDtypeStruct((width, depth), BF16),
            jax.ShapeDtypeStruct((width, rows), BF16),
        ),
        in_specs=[hbm, hbm, hbm, vmem, smem, smem],
        out_specs=(smem, vmem, vmem),
        scratch_shapes=[
            pltpu.VMEM((2, rows, depth), BF16),
            pltpu.VMEM((width, depth), BF16),
            pltpu.VMEM((3, 2, width, hr), BF16),
            pltpu.VMEM((3, 2, width, hr), BF16),
            pltpu.VMEM((width, rows), F32),
            pltpu.VMEM((width, rows), BF16),
            pltpu.VMEM((8, rows), F32),
            pltpu.VMEM((8, rows), F32),
            pltpu.VMEM((3, 8, rows), F32),
            pltpu.VMEM((3, 2, hr, rows), BF16),
            pltpu.VMEM((3, 2, hr, rows), BF16),
            pltpu.VMEM((3, 2, hr, rows), BF16),
            pltpu.VMEM((2, half, rows), BF16),
            pltpu.VMEM((2, half, rows), BF16),
            pltpu.VMEM((2, 8, rows), F32),
            pltpu.VMEM((NX, 8, rows), F32),
            pltpu.VMEM((NY, 8, rows), F32),
            pltpu.VMEM((NZ, 8, rows), F32),
            pltpu.VMEM((2, width, hr), F32),
            pltpu.VMEM((2, 2, width, hr), BF16),
            pltpu.VMEM((width, hr), BF16),
            pltpu.VMEM((width, hr), BF16),
            pltpu.VMEM((2, 2, width, hr), BF16),
            pltpu.VMEM((8, rows), F32),
            pltpu.VMEM((8, rows), F32),
            *buffers,
            pltpu.VMEM((half, depth), F32),
            pltpu.VMEM((width, hr), BF16),
            pltpu.SemaphoreType.DMA((1,)),
            pltpu.SemaphoreType.DMA((1,)),
            pltpu.SemaphoreType.DMA((4,)),
            pltpu.SemaphoreType.DMA((5,)),
            pltpu.SemaphoreType.DMA((2, 2)),
            pltpu.SemaphoreType.DMA((3, 2)),
            pltpu.SemaphoreType.DMA((3, 2)),
            pltpu.SemaphoreType.DMA((3,)),
            pltpu.SemaphoreType.DMA((2, 2)),
            pltpu.SemaphoreType.DMA((N_COPIES,)),
            pltpu.SemaphoreType.DMA((N_COPIES,)),
        ],
        compiler_params=pltpu.CompilerParams(
            collective_id=0, has_side_effects=True, vmem_limit_bytes=56 * 1024 * 1024
        ),
    )
    loss, grad, cap = call(x_rows, w_half.T, t_half.T, matched.reshape(1, rows), sharpness, offset)
    return (loss, grad.T, cap.T)


def solution(mesh):
    placed = (P("dp", None), P(None, "mp"), P("dp", "mp"), P("dp"), P(), P())
    return jax.shard_map(
        local,
        mesh=mesh,
        in_specs=placed,
        out_specs=(P(), P(None, "mp"), P("dp", "mp")),
        check_vma=False,
    )
```

```python
import jax
import jax.numpy as jnp
from jax import lax
from jax.experimental import pallas as pl
from jax.experimental.pallas import tpu as pltpu
from jax.sharding import PartitionSpec as P

STEPS = 2
NX, NY, NZ = 4, 8, 4
BLOCKS = NX * NY * NZ * 2
EPSILON = 1e-06
ROW_TILE = 16
LANES = 128
N_COPIES = 128
MESH = pl.DeviceIdType.MESH
F32, BF16 = jnp.float32, jnp.bfloat16


def dot(a, b, over_a, over_b):
    return lax.dot_general(a, b, (((over_a,), (over_b,)), ((), ())), preferred_element_type=F32)


def groups_of(width, depth):
    half, tiles = width // 2, depth // LANES
    one, two = tiles * 4 // 9, tiles * 7 // 9
    groups = []
    for first, last, order in ((0, one, "xyz"), (one, two, "yxz"), (two, tiles, "zxy")):
        counts = [{"x": NX, "y": NY, "z": NZ}[axis] for axis in order]
        held = [(last - first) * half]
        for count in counts[:2]:
            held.append(-(-held[-1] // (count * ROW_TILE)) * ROW_TILE)
        groups.append((first, last, order, counts, held))
    return groups


class Copies:
    def __init__(self, send_sem, recv_sem):
        self.send_sem, self.recv_sem, self.made = send_sem, recv_sem, []

    def start(self, source, target, device):
        i = len(self.made)
        copy = remote(source, target, self.send_sem.at[i], self.recv_sem.at[i], device)
        copy.start()
        self.made.append(copy)
        return copy


def remote(source, target, send_sem, recv_sem, device):
    return pltpu.make_async_remote_copy(
        src_ref=source,
        dst_ref=target,
        send_sem=send_sem,
        recv_sem=recv_sem,
        device_id=device,
        device_id_type=MESH,
    )


def rows_of(ref, place, count):
    return ref.at[pl.ds(pl.multiple_of(place * count, ROW_TILE), count)]


def kernel(
    x_hbm,
    w_hbm,
    t_hbm,
    matched_hbm,
    scale_hbm,
    offset_hbm,
    loss_ref,
    grad_hbm,
    cap_hbm,
    x_all,
    w_ref,
    text_raw,
    text_low,
    image_unit,
    image_low,
    sums_out,
    sums_in,
    text_sums,
    cos_out,
    cos_in,
    weight,
    back,
    back_all,
    loss_core,
    loss_x,
    loss_y,
    loss_z,
    text_dir,
    text_part,
    presum_in,
    presum_out,
    text_in,
    tdot_out,
    tdot_in,
    *rest,
):
    *buffers, cap_out, out_sem, grad_own, matched_ref, scale_ref, offset_ref, passed, passed_send, passed_recv, load_sem, text_send, text_recv, cos_send, cos_recv, part_send, part_recv, send_sem, recv_sem = rest
    width, rows = t_hbm.shape
    depth = x_hbm.shape[1]
    half, hr = width // 2, rows // 2
    dp, mp = lax.axis_index("dp"), lax.axis_index("mp")
    core = lax.rem(dp, 2)
    at = {"x": lax.rem(dp // 2, NX), "y": lax.rem(dp // (2 * NX), NY), "z": dp // (2 * NX * NY)}
    counts = {"x": NX, "y": NY, "z": NZ}
    strides = {"x": 2, "y": 2 * NX, "z": 2 * NX * NY}
    other_mp = (dp, 1 - mp)
    other_core = (dp + 1 - 2 * core, mp)

    def along_dp(step):
        return (lax.rem(dp + step + 2 * BLOCKS, BLOCKS), mp)

    def others(axis):
        places = [lax.rem(at[axis] + k, counts[axis]) for k in range(1, counts[axis])]
        return [(place, (dp + (place - at[axis]) * strides[axis], mp)) for place in places]

    def source_of(axis, k):
        return lax.rem(at[axis] - k + counts[axis], counts[axis])

    halves = [text_raw.at[0, 0], text_raw.at[0, 1]]
    loads = [
        pltpu.make_async_copy(t_hbm.at[:, :hr], text_raw.at[0, 0], load_sem.at[0]),
        pltpu.make_async_copy(t_hbm.at[:, hr:], text_raw.at[0, 1], load_sem.at[1]),
        pltpu.make_async_copy(w_hbm, w_ref, load_sem.at[2]),
        pltpu.make_async_copy(x_hbm, x_all.at[core], load_sem.at[3]),
        pltpu.make_async_copy(matched_hbm, matched_ref, load_sem.at[4]),
        pltpu.make_async_copy(scale_hbm, scale_ref, load_sem.at[5]),
        pltpu.make_async_copy(offset_hbm, offset_ref, load_sem.at[6]),
    ]
    for load in loads:
        load.start()

    barrier = pltpu.get_barrier_semaphore()
    greeted = [other_mp, other_core] + [along_dp(s) for s in (-2, -1, 1, 2)]
    greeted += [device for axis in "xyz" for _, device in others(axis)]
    for device in greeted:
        pl.semaphore_signal(barrier, inc=1, device_id=device, device_id_type=MESH)

    chip, plane = 2 * NX, 2 * NX * NY
    corner = (at["x"] == NX - 1) & (at["y"] == NY - 1)
    landing = (at["x"] == 0) & (at["y"] == 0)
    via_z = corner & (core == 1)
    via_x = (at["x"] == 0) & (at["y"] == NY - 1) & (core == 0)
    via_y = (at["x"] == NX - 1) & (at["y"] == 1) & (core == 0)
    passes_on = via_z | via_x | via_y
    back_z, back_x, back_y = -plane, 2 * (NX - 1), (NY - 2) * chip - plane
    back_here = jnp.where(via_z, back_z, jnp.where(via_x, back_x, back_y))

    def greet(device):
        pl.semaphore_signal(barrier, inc=1, device_id=device, device_id_type=MESH)

    @pl.when(passes_on)
    def _():
        greet(along_dp(back_here))

    @pl.when(landing & (core == 0))
    def _():
        greet(along_dp(-2 - back_x))
        greet(along_dp(-2 - back_y))

    @pl.when(landing & (core == 1))
    def _():
        greet(along_dp(-2 - back_z))

    home_z = landing & (core == 1)
    home_x = (at["x"] == NX - 1) & (at["y"] == 0) & (core == 0)
    home_y = (at["x"] == 0) & (at["y"] == NY - 2) & (core == 0)
    passes_home = home_z | home_x | home_y
    from_here = -jnp.where(home_z, back_z, jnp.where(home_x, back_x, back_y))

    @pl.when(passes_home)
    def _():
        greet(along_dp(from_here))

    @pl.when(corner & (core == 0))
    def _():
        greet(along_dp(2 + back_x))
        greet(along_dp(2 + back_y))

    @pl.when(corner & (core == 1))
    def _():
        greet(along_dp(2 + back_z))

    more = jnp.where(passes_on, 1, 0) + jnp.where(corner, 2 - core, 0)
    more += jnp.where(passes_home, 1, 0) + jnp.where(landing, 2 - core, 0)
    for load in loads[:2]:
        load.wait()
    pl.semaphore_wait(barrier, len(greeted) + more)

    copies = Copies(send_sem, recv_sem)
    send = copies.start

    def text_copy(h, step, number):
        return remote(
            halves[h],
            text_raw.at[step, h],
            text_send.at[number],
            text_recv.at[step - 1, h],
            along_dp(step),
        )

    def text_away(h, back, number):
        return remote(halves[h], passed, text_send.at[number], passed_recv.at[0], along_dp(-back))

    straight = ~corner

    @pl.when((core == 1) | straight)
    def _():
        text_copy(0, 1, 0).start()

    @pl.when(straight)
    def _():
        text_copy(1, 2, 1).start()

    @pl.when((core == 0) & straight)
    def _():
        text_copy(0, 2, 2).start()
        text_copy(1, 1, 3).start()

    @pl.when((core == 1) & corner)
    def _():
        text_away(1, back_z, 1).start()

    @pl.when((core == 0) & corner)
    def _():
        text_away(0, back_x, 2).start()
        text_away(1, back_y, 1).start()
        text_copy(0, 1, 0).start()
        text_copy(1, 1, 3).start()

    pass_half = jnp.where(via_x, 0, 1)
    pass_on = remote(
        passed,
        text_raw.at[2, pass_half],
        passed_send.at[0],
        text_recv.at[1, pass_half],
        along_dp(back_here + 2),
    )

    def text_arrived(step, h):
        remote(halves[0], text_raw.at[step, h], text_send.at[4], text_recv.at[step - 1, h], other_core).wait_recv()

    relay = remote(
        text_raw.at[1 + core, core],
        text_raw.at[2 - core, core],
        text_send.at[4],
        text_recv.at[1 - core, core],
        other_core,
    )

    for load in loads[2:]:
        load.wait()
    x_there = send(x_all.at[core], x_all.at[core], other_core)
    image_raw = dot(w_ref[...], x_all[core], 1, 1)
    sums_out[0:1, :] = jnp.sum(image_raw * image_raw, axis=0, keepdims=True)
    for h in (0, 1):
        own_text = text_raw[0, h].astype(F32)
        sums_out[1:2, h * hr : (h + 1) * hr] = jnp.sum(own_text * own_text, axis=0, keepdims=True)
    sums_there = send(sums_out, sums_in, other_mp)

    @pl.when(passes_on)
    def _():
        remote(halves[0], passed, passed_send.at[0], passed_recv.at[0], other_core).wait_recv()
        pass_on.start()

    sums_there.wait_recv()
    sums = sums_out[...] + sums_in[...]
    image_scale = lax.rsqrt(sums[0:1, :] + EPSILON)
    text_scale = lax.rsqrt(sums[1:2, :] + EPSILON)
    text_sums[0] = sums
    text_sums_there = [send(text_sums.at[0], text_sums.at[s], along_dp(s)) for s in (1, 2)]
    unit = image_raw * image_scale
    image_unit[...] = unit
    image_low[...] = unit.astype(BF16)

    def cos_copy(s, h):
        return remote(cos_out.at[s, h], cos_in.at[s, h], cos_send.at[s, h], cos_recv.at[s, h], other_mp)

    def cosines(s, h):
        scale = lax.rsqrt(text_sums[s, 1:2, :] + EPSILON)
        if isinstance(h, int):
            scale = scale[:, h * hr : (h + 1) * hr]
        else:
            scale = jnp.where(h == 0, scale[:, :hr], scale[:, hr:])
        low = (text_raw[s, h].astype(F32) * scale).astype(BF16)
        text_low[s, h] = low
        cos_out[s, h] = dot(low, image_low[...], 0, 0).astype(BF16)
        cos_copy(s, h).start()

    cosines(0, 0)
    cosines(0, 1)
    for copy in text_sums_there:
        copy.wait_recv()
    units = [(1, 0), (2 - core, core), (2, 1), (1 + core, 1 - core)]
    for number, (s, h) in enumerate(units):
        text_arrived(s, h)
        if number in (0, 2):

            @pl.when(core == number // 2)
            def _():
                relay.start()

        cosines(s, h)

    sharpness, offset = scale_ref[0], offset_ref[0]
    loss_rows = jnp.zeros((1, rows), F32)
    along_unit = jnp.zeros((1, rows), F32)
    direction = jnp.zeros((width, rows), F32)
    for s, h in [(0, 0), (0, 1)] + units:
        cos_copy(s, h).wait_recv()
        cos = cos_out[s, h].astype(F32) + cos_in[s, h].astype(F32)
        first = lax.rem(dp - s + BLOCKS, BLOCKS) * rows + h * hr
        matched = first + lax.broadcasted_iota(jnp.int32, (hr, rows), 0) == matched_ref[...]
        logit = sharpness * cos + offset
        against = jnp.where(matched, -logit, logit)
        small = jnp.exp(-jnp.abs(against))
        loss_rows += jnp.sum(jnp.maximum(against, 0.0) + jnp.log1p(small), axis=0, keepdims=True)
        sigmoid = jnp.where(against >= 0.0, 1.0, small) / (1.0 + small)
        low = (jnp.where(matched, -sigmoid, sigmoid) * sharpness).astype(BF16)
        weight[s, h] = low
        along_unit += jnp.sum(low.astype(F32) * cos, axis=0, keepdims=True)
        direction += dot(text_low[s, h], low, 1, 0)

    image_back = ((direction - image_unit[...] * along_unit) * image_scale).astype(BF16)
    back[0] = image_back[:half]
    back[1] = image_back[half:]
    back_there = send(back.at[1 - core], back_all.at[core], other_core)
    back_all[core] = back[core]
    loss_core[core] = jnp.broadcast_to(loss_rows, (8, rows))
    loss_core_there = send(loss_core.at[core], loss_core.at[core], other_core)

    def text_parts(s, h):
        text_part[s - 1, h] = dot(image_low[...], weight[s, h], 1, 1).astype(BF16)

    shared, alone = 1 + core, 2 - core
    def part_copy(source, which, h, step, number):
        return remote(
            source, text_in.at[which, h], part_send.at[number], part_recv.at[which, h], along_dp(-step)
        )

    grad_own[...] = dot(back_all[core], x_all[core], 1, 0)
    x_there.wait_recv()
    back_there.wait_recv()
    theirs, x_theirs = back_all[1 - core], x_all[1 - core]
    groups = groups_of(width, depth)
    levels = []
    for g, (first, last, order, _, held) in enumerate(groups):
        full, sums_2, land_1, land_2, land_3, got_2, result = buffers[7 * g : 7 * g + 7]
        levels.append(([full, sums_2], [land_1, land_2, land_3], [result, got_2]))

    def scatter(g, level):
        _, _, order, _, held = groups[g]
        source, landing = levels[g][0][level], levels[g][1][level]
        return [
            send(rows_of(source, place, held[level + 1]), landing.at[k], device)
            for k, (place, device) in enumerate(others(order[level]))
        ]

    def scattered(g, level, there):
        _, _, order, _, held = groups[g]
        source, landing = levels[g][0][level], levels[g][1][level]
        total = rows_of(source, at[order[level]], held[level + 1])[...].astype(F32)
        for k, copy in enumerate(there):
            copy.wait_recv()
            total += landing[k].astype(F32)
        return total.astype(BF16)

    def padded(ref, count):
        if ref.shape[0] > count:
            ref[count:, :] = jnp.zeros((ref.shape[0] - count, LANES), BF16)

    def spread(landing, axis, value):
        landing[at[axis]] = value
        return [send(landing.at[at[axis]], landing.at[at[axis]], device) for _, device in others(axis)]

    def loss_sum(there, landing, axis):
        for copy in there:
            copy.wait_recv()
        total = landing[0]
        for k in range(1, counts[axis]):
            total += landing[k]
        return total

    there = []
    for g, (first, last, order, _, held) in enumerate(groups):
        full = levels[g][0][0]
        for k in range(first, last):
            cols = slice(k * LANES, (k + 1) * LANES)
            part = grad_own[:, cols] + dot(theirs, x_theirs[:, cols], 1, 0)
            full[(k - first) * half : (k - first + 1) * half, :] = part.astype(BF16)
        padded(full, held[0])
        there.append(scatter(g, 0))
    loss_core_there.wait_recv()
    loss_there = spread(loss_x, "x", loss_core[0] + loss_core[1])

    text_parts(shared, 1 - core)
    presum_there = send(text_part.at[core, 1 - core], presum_in, other_core)
    text_parts(shared, core)
    for h in (0, 1):
        text_parts(alone, h)
    for h in (0, 1):
        text_dir[h] = dot(image_low[...], weight[0, h], 1, 1)
    presum_there.wait_recv()
    presum_out[...] = (text_part[core, core].astype(F32) + presum_in[...].astype(F32)).astype(BF16)
    part_copies = [
        part_copy(text_part.at[1 - core, h], 1 - core, h, alone, h) for h in (0, 1)
    ] + [part_copy(presum_out, 0, core, shared, 2)]

    for g, (_, _, order, _, held) in enumerate(groups):
        target = levels[g][0][1]
        target[: held[1], :] = scattered(g, 0, there[g])
        padded(target, held[1])
        there[g] = scatter(g, 1)
    loss_there = spread(loss_y, "y", loss_sum(loss_there, loss_x, "x"))

    def part_away(source, back, number):
        return remote(source, passed, part_send.at[number], passed_recv.at[0], along_dp(back))

    @pl.when(~landing)
    def _():
        for copy in part_copies:
            copy.start()

    @pl.when(landing & (core == 0))
    def _():
        part_away(text_part.at[1, 0], back_x, 0).start()
        part_away(text_part.at[1, 1], back_y, 1).start()
        part_copies[2].start()

    @pl.when(landing & (core == 1))
    def _():
        part_copies[0].start()
        part_copies[1].start()
        part_away(presum_out, back_z, 2).start()

    home_which, home_half = jnp.where(home_z, 0, 1), jnp.where(home_x, 0, 1)
    pass_home = remote(
        passed,
        text_in.at[home_which, home_half],
        passed_send.at[0],
        part_recv.at[home_which, home_half],
        along_dp(from_here - 2),
    )
    for g, (_, _, order, _, held) in enumerate(groups):
        there[g] = spread(levels[g][1][2], order[2], scattered(g, 1, there[g]))
    loss_there = spread(loss_z, "z", loss_sum(loss_there, loss_y, "y"))

    @pl.when(passes_home)
    def _():
        remote(presum_out, passed, passed_send.at[0], passed_recv.at[0], other_core).wait_recv()
        pass_home.start()

    for g, (_, _, order, counts_g, held) in enumerate(groups):
        landing_g = levels[g][1][2]
        for copy in there[g]:
            copy.wait_recv()
        total = landing_g[0].astype(F32)
        for k in range(1, counts_g[2]):
            total += landing_g[k].astype(F32)
        own = rows_of(levels[g][2][1], at[order[1]], held[2])
        own[...] = total.astype(BF16)
        there[g] = [send(own, own, device) for _, device in others(order[1])]

    loss_now = loss_sum(loss_there, loss_z, "z")
    loss_ref[0] = jnp.sum(loss_now[0:1, :]) / (rows * BLOCKS)

    def chunk(g, place):
        return rows_of(levels[g][2][0].at[core], place, groups[g][4][1])

    relayed = [[] for _ in groups]
    for g, (_, _, order, _, held) in enumerate(groups):
        for copy in there[g]:
            copy.wait_recv()
        own = chunk(g, at[order[0]])
        own[...] = levels[g][2][1][: held[1], :]
        there[g] = [send(own, own, device) for _, device in others(order[0])]
        relayed[g].append(send(own, own, other_core))

    def part_arrived(which, h):
        part_copy(presum_out, which, h, 1, 2).wait_recv()

    for h in (0, 1):
        part_arrived(0, h)
        text_dir[h] += text_in[0, h].astype(F32)

    @pl.when(core == 0)
    def _():
        for h in (0, 1):
            part_arrived(1, h)
            text_dir[h] += text_in[1, h].astype(F32)

    def text_unit(h):
        return text_raw[0, h].astype(F32) * text_scale[:, h * hr : (h + 1) * hr]

    for h in (0, 1):
        tdot_out[:, h * hr : (h + 1) * hr] = jnp.broadcast_to(
            jnp.sum(text_unit(h) * text_dir[h], axis=0, keepdims=True), (8, hr)
        )
    tdot_there = send(tdot_out, tdot_in, other_mp)

    stored = []

    def store(g, of):
        first, last, _, _, _ = groups[g]
        for k in range(first, last):
            block = levels[g][2][0].at[of, (k - first) * half : (k - first + 1) * half]
            rows_k = pl.ds(pl.multiple_of(of * half, ROW_TILE), half)
            place = grad_hbm.at[rows_k, k * LANES : (k + 1) * LANES]
            stored.append(pltpu.make_async_copy(block, place, out_sem.at[len(stored)]))
            stored[-1].start()

    for g, (_, _, order, _, held) in enumerate(groups):
        for k, copy in enumerate(there[g]):
            copy.wait_recv()
            arrived = chunk(g, source_of(order[0], k + 1))
            relayed[g].append(send(arrived, arrived, other_core))
        store(g, core)
    tdot_there.wait_recv()
    tdot = tdot_out[0:1, :] + tdot_in[0:1, :]
    for h in (0, 1):
        lanes = slice(h * hr, (h + 1) * hr)
        cap_out[:, lanes] = (
            (text_dir[h] - text_unit(h) * tdot[:, lanes]) * text_scale[:, lanes]
        ).astype(BF16)
    stored.append(pltpu.make_async_copy(cap_out, cap_hbm, out_sem.at[len(stored)]))
    stored[-1].start()
    for g in range(len(groups)):
        for copy in relayed[g]:
            copy.wait_recv()
        store(g, 1 - core)
    for copy in stored:
        copy.wait()

    for copy in copies.made + [text_copy(0, 1, 0), text_copy(1, 2, 1), relay] + part_copies:
        copy.wait_send()

    @pl.when(core == 0)
    def _():
        for copy in (text_copy(0, 2, 2), text_copy(1, 1, 3)):
            copy.wait_send()

    @pl.when(passes_on)
    def _():
        pass_on.wait_send()

    @pl.when(passes_home)
    def _():
        pass_home.wait_send()

    for s in range(STEPS + 1):
        for h in (0, 1):
            cos_copy(s, h).wait_send()


def local(x_rows, w_half, t_half, matched, sharpness, offset):
    rows, depth = x_rows.shape
    width = w_half.shape[1]
    half, hr = width // 2, rows // 2
    hbm = pl.BlockSpec(memory_space=pltpu.HBM)
    smem = pl.BlockSpec(memory_space=pltpu.SMEM)
    buffers = []
    for _, _, _, (n1, n2, n3), (_, r1, r2) in groups_of(width, depth):
        buffers += [
            pltpu.VMEM((n1 * r1, LANES), BF16),
            pltpu.VMEM((n2 * r2, LANES), BF16),
            pltpu.VMEM((n1 - 1, r1, LANES), BF16),
            pltpu.VMEM((n2 - 1, r2, LANES), BF16),
            pltpu.VMEM((n3, r2, LANES), BF16),
            pltpu.VMEM((n2 * r2, LANES), BF16),
            pltpu.VMEM((2, n1 * r1, LANES), BF16),
        ]
    call = pl.pallas_call(
        kernel,
        out_shape=(
            jax.ShapeDtypeStruct((1,), F32),
            jax.ShapeDtypeStruct((width, depth), BF16),
            jax.ShapeDtypeStruct((width, rows), BF16),
        ),
        in_specs=[hbm] * 6,
        out_specs=(smem, hbm, hbm),
        scratch_shapes=[
            pltpu.VMEM((2, rows, depth), BF16),
            pltpu.VMEM((width, depth), BF16),
            pltpu.VMEM((3, 2, width, hr), BF16),
            pltpu.VMEM((3, 2, width, hr), BF16),
            pltpu.VMEM((width, rows), F32),
            pltpu.VMEM((width, rows), BF16),
            pltpu.VMEM((8, rows), F32),
            pltpu.VMEM((8, rows), F32),
            pltpu.VMEM((3, 8, rows), F32),
            pltpu.VMEM((3, 2, hr, rows), BF16),
            pltpu.VMEM((3, 2, hr, rows), BF16),
            pltpu.VMEM((3, 2, hr, rows), BF16),
            pltpu.VMEM((2, half, rows), BF16),
            pltpu.VMEM((2, half, rows), BF16),
            pltpu.VMEM((2, 8, rows), F32),
            pltpu.VMEM((NX, 8, rows), F32),
            pltpu.VMEM((NY, 8, rows), F32),
            pltpu.VMEM((NZ, 8, rows), F32),
            pltpu.VMEM((2, width, hr), F32),
            pltpu.VMEM((2, 2, width, hr), BF16),
            pltpu.VMEM((width, hr), BF16),
            pltpu.VMEM((width, hr), BF16),
            pltpu.VMEM((2, 2, width, hr), BF16),
            pltpu.VMEM((8, rows), F32),
            pltpu.VMEM((8, rows), F32),
            *buffers,
            pltpu.VMEM((width, rows), BF16),
            pltpu.SemaphoreType.DMA((2 * depth // LANES + 1,)),
            pltpu.VMEM((half, depth), F32),
            pltpu.VMEM((1, rows), jnp.int32),
            pltpu.SMEM((1,), F32),
            pltpu.SMEM((1,), F32),
            pltpu.VMEM((width, hr), BF16),
            pltpu.SemaphoreType.DMA((1,)),
            pltpu.SemaphoreType.DMA((1,)),
            pltpu.SemaphoreType.DMA((7,)),
            pltpu.SemaphoreType.DMA((5,)),
            pltpu.SemaphoreType.DMA((2, 2)),
            pltpu.SemaphoreType.DMA((3, 2)),
            pltpu.SemaphoreType.DMA((3, 2)),
            pltpu.SemaphoreType.DMA((3,)),
            pltpu.SemaphoreType.DMA((2, 2)),
            pltpu.SemaphoreType.DMA((N_COPIES,)),
            pltpu.SemaphoreType.DMA((N_COPIES,)),
        ],
        compiler_params=pltpu.CompilerParams(
            collective_id=0, has_side_effects=True, vmem_limit_bytes=56 * 1024 * 1024
        ),
    )
    loss, grad, cap = call(x_rows, w_half.T, t_half.T, matched.reshape(1, rows), sharpness, offset)
    return (loss, grad.T, cap.T)


def solution(mesh):
    placed = (P("dp", None), P(None, "mp"), P("dp", "mp"), P("dp"), P(), P())
    return jax.shard_map(
        local,
        mesh=mesh,
        in_specs=placed,
        out_specs=(P(), P(None, "mp"), P("dp", "mp")),
        check_vma=False,
    )
```

```python
import jax
import jax.numpy as jnp
from jax import lax
from jax.experimental import pallas as pl
from jax.experimental.pallas import tpu as pltpu
from jax.sharding import PartitionSpec as P

STEPS = 2
NX, NY, NZ = 4, 8, 4
BLOCKS = NX * NY * NZ * 2
EPSILON = 1e-06
ROW_TILE = 16
LANES = 128
N_COPIES = 128
MESH = pl.DeviceIdType.MESH
F32, BF16 = jnp.float32, jnp.bfloat16


def dot(a, b, over_a, over_b):
    return lax.dot_general(a, b, (((over_a,), (over_b,)), ((), ())), preferred_element_type=F32)


def groups_of(width, depth):
    half, tiles = width // 2, depth // LANES
    one, two = tiles * 4 // 9, tiles * 7 // 9
    groups = []
    for first, last, order in ((0, one, "xyz"), (one, two, "yxz"), (two, tiles, "zxy")):
        counts = [{"x": NX, "y": NY, "z": NZ}[axis] for axis in order]
        held = [(last - first) * half]
        for count in counts[:2]:
            held.append(-(-held[-1] // (count * ROW_TILE)) * ROW_TILE)
        groups.append((first, last, order, counts, held))
    return groups


class Copies:
    def __init__(self, send_sem, recv_sem):
        self.send_sem, self.recv_sem, self.made = send_sem, recv_sem, []

    def start(self, source, target, device):
        i = len(self.made)
        copy = remote(source, target, self.send_sem.at[i], self.recv_sem.at[i], device)
        copy.start()
        self.made.append(copy)
        return copy


def remote(source, target, send_sem, recv_sem, device):
    return pltpu.make_async_remote_copy(
        src_ref=source,
        dst_ref=target,
        send_sem=send_sem,
        recv_sem=recv_sem,
        device_id=device,
        device_id_type=MESH,
    )


def rows_of(ref, place, count):
    return ref.at[pl.ds(pl.multiple_of(place * count, ROW_TILE), count)]


def kernel(
    x_hbm,
    w_hbm,
    t_hbm,
    matched_hbm,
    scale_hbm,
    offset_hbm,
    loss_ref,
    grad_hbm,
    cap_hbm,
    x_all,
    w_ref,
    text_raw,
    text_low,
    image_unit,
    image_low,
    sums_out,
    sums_in,
    text_sums,
    cos_out,
    cos_in,
    weight,
    back,
    back_all,
    loss_core,
    loss_x,
    loss_y,
    loss_z,
    text_dir,
    text_part,
    presum_in,
    presum_out,
    text_in,
    tdot_out,
    tdot_in,
    *rest,
):
    *buffers, image_dir, cap_out, out_sem, grad_own, matched_ref, scale_ref, offset_ref, passed, passed_send, passed_recv, load_sem, text_send, text_recv, cos_send, cos_recv, part_send, part_recv, send_sem, recv_sem = rest
    width, rows = t_hbm.shape
    depth = x_hbm.shape[1]
    half, hr = width // 2, rows // 2
    dp, mp = lax.axis_index("dp"), lax.axis_index("mp")
    core = lax.rem(dp, 2)
    at = {"x": lax.rem(dp // 2, NX), "y": lax.rem(dp // (2 * NX), NY), "z": dp // (2 * NX * NY)}
    counts = {"x": NX, "y": NY, "z": NZ}
    strides = {"x": 2, "y": 2 * NX, "z": 2 * NX * NY}
    other_mp = (dp, 1 - mp)
    other_core = (dp + 1 - 2 * core, mp)

    def along_dp(step):
        return (lax.rem(dp + step + 2 * BLOCKS, BLOCKS), mp)

    def others(axis):
        places = [lax.rem(at[axis] + k, counts[axis]) for k in range(1, counts[axis])]
        return [(place, (dp + (place - at[axis]) * strides[axis], mp)) for place in places]

    def source_of(axis, k):
        return lax.rem(at[axis] - k + counts[axis], counts[axis])

    halves = [text_raw.at[0, 0], text_raw.at[0, 1]]
    loads = [
        pltpu.make_async_copy(t_hbm.at[:, :hr], text_raw.at[0, 0], load_sem.at[0]),
        pltpu.make_async_copy(t_hbm.at[:, hr:], text_raw.at[0, 1], load_sem.at[1]),
        pltpu.make_async_copy(w_hbm, w_ref, load_sem.at[2]),
        pltpu.make_async_copy(x_hbm, x_all.at[core], load_sem.at[3]),
        pltpu.make_async_copy(matched_hbm, matched_ref, load_sem.at[4]),
        pltpu.make_async_copy(scale_hbm, scale_ref, load_sem.at[5]),
        pltpu.make_async_copy(offset_hbm, offset_ref, load_sem.at[6]),
    ]
    for load in loads:
        load.start()

    barrier = pltpu.get_barrier_semaphore()
    greeted = [other_mp, other_core] + [along_dp(s) for s in (-2, -1, 1, 2)]
    greeted += [device for axis in "xyz" for _, device in others(axis)]
    for device in greeted:
        pl.semaphore_signal(barrier, inc=1, device_id=device, device_id_type=MESH)

    chip, plane = 2 * NX, 2 * NX * NY
    corner = (at["x"] == NX - 1) & (at["y"] == NY - 1)
    landing = (at["x"] == 0) & (at["y"] == 0)
    via_z = corner & (core == 1)
    via_x = (at["x"] == 0) & (at["y"] == NY - 1) & (core == 0)
    via_y = (at["x"] == NX - 1) & (at["y"] == 1) & (core == 0)
    passes_on = via_z | via_x | via_y
    back_z, back_x, back_y = -plane, 2 * (NX - 1), (NY - 2) * chip - plane
    back_here = jnp.where(via_z, back_z, jnp.where(via_x, back_x, back_y))

    def greet(device):
        pl.semaphore_signal(barrier, inc=1, device_id=device, device_id_type=MESH)

    @pl.when(passes_on)
    def _():
        greet(along_dp(back_here))

    @pl.when(landing & (core == 0))
    def _():
        greet(along_dp(-2 - back_x))
        greet(along_dp(-2 - back_y))

    @pl.when(landing & (core == 1))
    def _():
        greet(along_dp(-2 - back_z))

    home_z = landing & (core == 1)
    home_x = (at["x"] == NX - 1) & (at["y"] == 0) & (core == 0)
    home_y = (at["x"] == 0) & (at["y"] == NY - 2) & (core == 0)
    passes_home = home_z | home_x | home_y
    from_here = -jnp.where(home_z, back_z, jnp.where(home_x, back_x, back_y))

    @pl.when(passes_home)
    def _():
        greet(along_dp(from_here))

    @pl.when(corner & (core == 0))
    def _():
        greet(along_dp(2 + back_x))
        greet(along_dp(2 + back_y))

    @pl.when(corner & (core == 1))
    def _():
        greet(along_dp(2 + back_z))

    more = jnp.where(passes_on, 1, 0) + jnp.where(corner, 2 - core, 0)
    more += jnp.where(passes_home, 1, 0) + jnp.where(landing, 2 - core, 0)
    for load in loads[:2]:
        load.wait()
    pl.semaphore_wait(barrier, len(greeted) + more)

    copies = Copies(send_sem, recv_sem)
    send = copies.start

    def text_copy(h, step, number):
        return remote(
            halves[h],
            text_raw.at[step, h],
            text_send.at[number],
            text_recv.at[step - 1, h],
            along_dp(step),
        )

    def text_away(h, back, number):
        return remote(halves[h], passed, text_send.at[number], passed_recv.at[0], along_dp(-back))

    straight = ~corner

    @pl.when((core == 1) | straight)
    def _():
        text_copy(0, 1, 0).start()

    @pl.when(straight)
    def _():
        text_copy(1, 2, 1).start()

    @pl.when((core == 0) & straight)
    def _():
        text_copy(0, 2, 2).start()
        text_copy(1, 1, 3).start()

    @pl.when((core == 1) & corner)
    def _():
        text_away(1, back_z, 1).start()

    @pl.when((core == 0) & corner)
    def _():
        text_away(0, back_x, 2).start()
        text_away(1, back_y, 1).start()
        text_copy(0, 1, 0).start()
        text_copy(1, 1, 3).start()

    pass_half = jnp.where(via_x, 0, 1)
    pass_on = remote(
        passed,
        text_raw.at[2, pass_half],
        passed_send.at[0],
        text_recv.at[1, pass_half],
        along_dp(back_here + 2),
    )

    def text_arrived(step, h):
        remote(halves[0], text_raw.at[step, h], text_send.at[4], text_recv.at[step - 1, h], other_core).wait_recv()

    relay = remote(
        text_raw.at[1 + core, core],
        text_raw.at[2 - core, core],
        text_send.at[4],
        text_recv.at[1 - core, core],
        other_core,
    )

    for load in loads[2:]:
        load.wait()
    x_there = send(x_all.at[core], x_all.at[core], other_core)
    image_raw = dot(w_ref[...], x_all[core], 1, 1)
    sums_out[0:1, :] = jnp.sum(image_raw * image_raw, axis=0, keepdims=True)
    for h in (0, 1):
        own_text = text_raw[0, h].astype(F32)
        sums_out[1:2, h * hr : (h + 1) * hr] = jnp.sum(own_text * own_text, axis=0, keepdims=True)
    sums_there = send(sums_out, sums_in, other_mp)

    @pl.when(passes_on)
    def _():
        remote(halves[0], passed, passed_send.at[0], passed_recv.at[0], other_core).wait_recv()
        pass_on.start()

    sums_there.wait_recv()
    sums = sums_out[...] + sums_in[...]
    image_scale = lax.rsqrt(sums[0:1, :] + EPSILON)
    text_scale = lax.rsqrt(sums[1:2, :] + EPSILON)
    text_sums[0] = sums
    text_sums_there = [send(text_sums.at[0], text_sums.at[s], along_dp(s)) for s in (1, 2)]
    unit = image_raw * image_scale
    image_unit[...] = unit
    image_low[...] = unit.astype(BF16)

    def cos_copy(s, h):
        return remote(cos_out.at[s, h], cos_in.at[s, h], cos_send.at[s, h], cos_recv.at[s, h], other_mp)

    def cosines(s, h):
        scale = lax.rsqrt(text_sums[s, 1:2, :] + EPSILON)
        if isinstance(h, int):
            scale = scale[:, h * hr : (h + 1) * hr]
        else:
            scale = jnp.where(h == 0, scale[:, :hr], scale[:, hr:])
        low = (text_raw[s, h].astype(F32) * scale).astype(BF16)
        text_low[s, h] = low
        cos_out[s, h] = dot(low, image_low[...], 0, 0).astype(BF16)
        cos_copy(s, h).start()

    cosines(0, 0)
    cosines(0, 1)
    for copy in text_sums_there:
        copy.wait_recv()
    units = [(1, 0), (2 - core, core), (2, 1), (1 + core, 1 - core)]
    for number, (s, h) in enumerate(units):
        text_arrived(s, h)
        if number in (0, 2):

            @pl.when(core == number // 2)
            def _():
                relay.start()

        cosines(s, h)

    sharpness, offset = scale_ref[0], offset_ref[0]
    loss_rows = jnp.zeros((1, rows), F32)
    along_unit = jnp.zeros((1, rows), F32)
    direction = jnp.zeros((width, rows), F32)
    for s, h in [(0, 0), (0, 1)] + units:
        cos_copy(s, h).wait_recv()
        cos = cos_out[s, h].astype(F32) + cos_in[s, h].astype(F32)
        first = lax.rem(dp - s + BLOCKS, BLOCKS) * rows + h * hr
        matched = first + lax.broadcasted_iota(jnp.int32, (hr, rows), 0) == matched_ref[...]
        logit = sharpness * cos + offset
        against = jnp.where(matched, -logit, logit)
        small = jnp.exp(-jnp.abs(against))
        loss_rows += jnp.sum(jnp.maximum(against, 0.0) + jnp.log1p(small), axis=0, keepdims=True)
        sigmoid = jnp.where(against >= 0.0, 1.0, small) / (1.0 + small)
        low = (jnp.where(matched, -sigmoid, sigmoid) * sharpness).astype(BF16)
        weight[s, h] = low
        along_unit += jnp.sum(low.astype(F32) * cos, axis=0, keepdims=True)
        direction += dot(text_low[s, h], low, 1, 0)

    image_dir[...] = direction

    def image_back(of):
        rows_h = pl.ds(pl.multiple_of(of * half, ROW_TILE), half)
        return ((image_dir[rows_h, :] - image_unit[rows_h, :] * along_unit) * image_scale).astype(BF16)

    back[...] = image_back(1 - core)
    back_there = send(back, back_all.at[core], other_core)
    back_all[core] = image_back(core)
    loss_core[core] = jnp.broadcast_to(loss_rows, (8, rows))
    loss_core_there = send(loss_core.at[core], loss_core.at[core], other_core)

    def text_parts(s, h):
        text_part[s - 1, h] = dot(image_low[...], weight[s, h], 1, 1).astype(BF16)

    shared, alone = 1 + core, 2 - core
    def part_copy(source, which, h, step, number):
        return remote(
            source, text_in.at[which, h], part_send.at[number], part_recv.at[which, h], along_dp(-step)
        )

    grad_own[...] = dot(back_all[core], x_all[core], 1, 0)
    x_there.wait_recv()
    back_there.wait_recv()
    theirs, x_theirs = back_all[1 - core], x_all[1 - core]
    groups = groups_of(width, depth)
    levels = []
    for g, (first, last, order, _, held) in enumerate(groups):
        full, sums_2, land_1, land_2, land_3, got_2, result = buffers[7 * g : 7 * g + 7]
        levels.append(([full, sums_2], [land_1, land_2, land_3], [result, got_2]))

    def scatter(g, level):
        _, _, order, _, held = groups[g]
        source, landing = levels[g][0][level], levels[g][1][level]
        return [
            send(rows_of(source, place, held[level + 1]), landing.at[k], device)
            for k, (place, device) in enumerate(others(order[level]))
        ]

    def scattered(g, level, there):
        _, _, order, _, held = groups[g]
        source, landing = levels[g][0][level], levels[g][1][level]
        total = rows_of(source, at[order[level]], held[level + 1])[...].astype(F32)
        for k, copy in enumerate(there):
            copy.wait_recv()
            total += landing[k].astype(F32)
        return total.astype(BF16)

    def padded(ref, count):
        if ref.shape[0] > count:
            ref[count:, :] = jnp.zeros((ref.shape[0] - count, LANES), BF16)

    def spread(landing, axis, value):
        landing[at[axis]] = value
        return [send(landing.at[at[axis]], landing.at[at[axis]], device) for _, device in others(axis)]

    def loss_sum(there, landing, axis):
        for copy in there:
            copy.wait_recv()
        total = landing[0]
        for k in range(1, counts[axis]):
            total += landing[k]
        return total

    there = []
    for g, (first, last, order, _, held) in enumerate(groups):
        full = levels[g][0][0]
        for k in range(first, last):
            cols = slice(k * LANES, (k + 1) * LANES)
            part = grad_own[:, cols] + dot(theirs, x_theirs[:, cols], 1, 0)
            full[(k - first) * half : (k - first + 1) * half, :] = part.astype(BF16)
        padded(full, held[0])
        there.append(scatter(g, 0))
    loss_core_there.wait_recv()
    loss_there = spread(loss_x, "x", loss_core[0] + loss_core[1])

    text_parts(shared, 1 - core)
    presum_there = send(text_part.at[core, 1 - core], presum_in, other_core)
    text_parts(shared, core)
    for h in (0, 1):
        text_parts(alone, h)
    for h in (0, 1):
        text_dir[h] = dot(image_low[...], weight[0, h], 1, 1)
    presum_there.wait_recv()
    presum_out[...] = (text_part[core, core].astype(F32) + presum_in[...].astype(F32)).astype(BF16)
    part_copies = [
        part_copy(text_part.at[1 - core, h], 1 - core, h, alone, h) for h in (0, 1)
    ] + [part_copy(presum_out, 0, core, shared, 2)]

    for g, (_, _, order, _, held) in enumerate(groups):
        target = levels[g][0][1]
        target[: held[1], :] = scattered(g, 0, there[g])
        padded(target, held[1])
        there[g] = scatter(g, 1)
    loss_there = spread(loss_y, "y", loss_sum(loss_there, loss_x, "x"))

    def part_away(source, back, number):
        return remote(source, passed, part_send.at[number], passed_recv.at[0], along_dp(back))

    @pl.when(~landing)
    def _():
        for copy in part_copies:
            copy.start()

    @pl.when(landing & (core == 0))
    def _():
        part_away(text_part.at[1, 0], back_x, 0).start()
        part_away(text_part.at[1, 1], back_y, 1).start()
        part_copies[2].start()

    @pl.when(landing & (core == 1))
    def _():
        part_copies[0].start()
        part_copies[1].start()
        part_away(presum_out, back_z, 2).start()

    home_which, home_half = jnp.where(home_z, 0, 1), jnp.where(home_x, 0, 1)
    pass_home = remote(
        passed,
        text_in.at[home_which, home_half],
        passed_send.at[0],
        part_recv.at[home_which, home_half],
        along_dp(from_here - 2),
    )
    for g, (_, _, order, _, held) in enumerate(groups):
        there[g] = spread(levels[g][1][2], order[2], scattered(g, 1, there[g]))
    loss_there = spread(loss_z, "z", loss_sum(loss_there, loss_y, "y"))

    @pl.when(passes_home)
    def _():
        remote(presum_out, passed, passed_send.at[0], passed_recv.at[0], other_core).wait_recv()
        pass_home.start()

    for g, (_, _, order, counts_g, held) in enumerate(groups):
        landing_g = levels[g][1][2]
        for copy in there[g]:
            copy.wait_recv()
        total = landing_g[0].astype(F32)
        for k in range(1, counts_g[2]):
            total += landing_g[k].astype(F32)
        own = rows_of(levels[g][2][1], at[order[1]], held[2])
        own[...] = total.astype(BF16)
        there[g] = [send(own, own, device) for _, device in others(order[1])]

    loss_now = loss_sum(loss_there, loss_z, "z")
    loss_ref[0] = jnp.sum(loss_now[0:1, :]) / (rows * BLOCKS)

    def chunk(g, place):
        return rows_of(levels[g][2][0].at[core], place, groups[g][4][1])

    relayed = [[] for _ in groups]
    for g, (_, _, order, _, held) in enumerate(groups):
        for copy in there[g]:
            copy.wait_recv()
        own = chunk(g, at[order[0]])
        own[...] = levels[g][2][1][: held[1], :]
        there[g] = [send(own, own, device) for _, device in others(order[0])]
        relayed[g].append(send(own, own, other_core))

    def part_arrived(which, h):
        part_copy(presum_out, which, h, 1, 2).wait_recv()

    for h in (0, 1):
        part_arrived(0, h)
        text_dir[h] += text_in[0, h].astype(F32)

    @pl.when(core == 0)
    def _():
        for h in (0, 1):
            part_arrived(1, h)
            text_dir[h] += text_in[1, h].astype(F32)

    def text_unit(h):
        return text_raw[0, h].astype(F32) * text_scale[:, h * hr : (h + 1) * hr]

    for h in (0, 1):
        tdot_out[:, h * hr : (h + 1) * hr] = jnp.broadcast_to(
            jnp.sum(text_unit(h) * text_dir[h], axis=0, keepdims=True), (8, hr)
        )
    tdot_there = send(tdot_out, tdot_in, other_mp)

    stored = []

    def store(g, of):
        first, last, _, _, _ = groups[g]
        for k in range(first, last):
            block = levels[g][2][0].at[of, (k - first) * half : (k - first + 1) * half]
            rows_k = pl.ds(pl.multiple_of(of * half, ROW_TILE), half)
            place = grad_hbm.at[rows_k, k * LANES : (k + 1) * LANES]
            stored.append(pltpu.make_async_copy(block, place, out_sem.at[len(stored)]))
            stored[-1].start()

    for g, (_, _, order, _, held) in enumerate(groups):
        for k, copy in enumerate(there[g]):
            copy.wait_recv()
            arrived = chunk(g, source_of(order[0], k + 1))
            relayed[g].append(send(arrived, arrived, other_core))
        store(g, core)
    tdot_there.wait_recv()
    tdot = tdot_out[0:1, :] + tdot_in[0:1, :]
    for h in (0, 1):
        lanes = slice(h * hr, (h + 1) * hr)
        cap_out[:, lanes] = (
            (text_dir[h] - text_unit(h) * tdot[:, lanes]) * text_scale[:, lanes]
        ).astype(BF16)
    stored.append(pltpu.make_async_copy(cap_out, cap_hbm, out_sem.at[len(stored)]))
    stored[-1].start()
    for g in range(len(groups)):
        for copy in relayed[g]:
            copy.wait_recv()
        store(g, 1 - core)
    for copy in stored:
        copy.wait()

    for copy in copies.made + [text_copy(0, 1, 0), text_copy(1, 2, 1), relay] + part_copies:
        copy.wait_send()

    @pl.when(core == 0)
    def _():
        for copy in (text_copy(0, 2, 2), text_copy(1, 1, 3)):
            copy.wait_send()

    @pl.when(passes_on)
    def _():
        pass_on.wait_send()

    @pl.when(passes_home)
    def _():
        pass_home.wait_send()

    for s in range(STEPS + 1):
        for h in (0, 1):
            cos_copy(s, h).wait_send()


def local(x_rows, w_half, t_half, matched, sharpness, offset):
    rows, depth = x_rows.shape
    width = w_half.shape[1]
    half, hr = width // 2, rows // 2
    hbm = pl.BlockSpec(memory_space=pltpu.HBM)
    smem = pl.BlockSpec(memory_space=pltpu.SMEM)
    buffers = []
    for _, _, _, (n1, n2, n3), (_, r1, r2) in groups_of(width, depth):
        buffers += [
            pltpu.VMEM((n1 * r1, LANES), BF16),
            pltpu.VMEM((n2 * r2, LANES), BF16),
            pltpu.VMEM((n1 - 1, r1, LANES), BF16),
            pltpu.VMEM((n2 - 1, r2, LANES), BF16),
            pltpu.VMEM((n3, r2, LANES), BF16),
            pltpu.VMEM((n2 * r2, LANES), BF16),
            pltpu.VMEM((2, n1 * r1, LANES), BF16),
        ]
    call = pl.pallas_call(
        kernel,
        out_shape=(
            jax.ShapeDtypeStruct((1,), F32),
            jax.ShapeDtypeStruct((width, depth), BF16),
            jax.ShapeDtypeStruct((width, rows), BF16),
        ),
        in_specs=[hbm] * 6,
        out_specs=(smem, hbm, hbm),
        scratch_shapes=[
            pltpu.VMEM((2, rows, depth), BF16),
            pltpu.VMEM((width, depth), BF16),
            pltpu.VMEM((3, 2, width, hr), BF16),
            pltpu.VMEM((3, 2, width, hr), BF16),
            pltpu.VMEM((width, rows), F32),
            pltpu.VMEM((width, rows), BF16),
            pltpu.VMEM((8, rows), F32),
            pltpu.VMEM((8, rows), F32),
            pltpu.VMEM((3, 8, rows), F32),
            pltpu.VMEM((3, 2, hr, rows), BF16),
            pltpu.VMEM((3, 2, hr, rows), BF16),
            pltpu.VMEM((3, 2, hr, rows), BF16),
            pltpu.VMEM((half, rows), BF16),
            pltpu.VMEM((2, half, rows), BF16),
            pltpu.VMEM((2, 8, rows), F32),
            pltpu.VMEM((NX, 8, rows), F32),
            pltpu.VMEM((NY, 8, rows), F32),
            pltpu.VMEM((NZ, 8, rows), F32),
            pltpu.VMEM((2, width, hr), F32),
            pltpu.VMEM((2, 2, width, hr), BF16),
            pltpu.VMEM((width, hr), BF16),
            pltpu.VMEM((width, hr), BF16),
            pltpu.VMEM((2, 2, width, hr), BF16),
            pltpu.VMEM((8, rows), F32),
            pltpu.VMEM((8, rows), F32),
            *buffers,
            pltpu.VMEM((width, rows), F32),
            pltpu.VMEM((width, rows), BF16),
            pltpu.SemaphoreType.DMA((2 * depth // LANES + 1,)),
            pltpu.VMEM((half, depth), F32),
            pltpu.VMEM((1, rows), jnp.int32),
            pltpu.SMEM((1,), F32),
            pltpu.SMEM((1,), F32),
            pltpu.VMEM((width, hr), BF16),
            pltpu.SemaphoreType.DMA((1,)),
            pltpu.SemaphoreType.DMA((1,)),
            pltpu.SemaphoreType.DMA((7,)),
            pltpu.SemaphoreType.DMA((5,)),
            pltpu.SemaphoreType.DMA((2, 2)),
            pltpu.SemaphoreType.DMA((3, 2)),
            pltpu.SemaphoreType.DMA((3, 2)),
            pltpu.SemaphoreType.DMA((3,)),
            pltpu.SemaphoreType.DMA((2, 2)),
            pltpu.SemaphoreType.DMA((N_COPIES,)),
            pltpu.SemaphoreType.DMA((N_COPIES,)),
        ],
        compiler_params=pltpu.CompilerParams(
            collective_id=0, has_side_effects=True, vmem_limit_bytes=56 * 1024 * 1024
        ),
    )
    loss, grad, cap = call(x_rows, w_half.T, t_half.T, matched.reshape(1, rows), sharpness, offset)
    return (loss, grad.T, cap.T)


def solution(mesh):
    placed = (P("dp", None), P(None, "mp"), P("dp", "mp"), P("dp"), P(), P())
    return jax.shard_map(
        local,
        mesh=mesh,
        in_specs=placed,
        out_specs=(P(), P(None, "mp"), P("dp", "mp")),
        check_vma=False,
    )
```
